512 devices in a mesh: dp: 128 (over z, y, core), owner: 4 (over x).
Axes of the slice: x: 4, y: 8, z: 8, core: 2. Of those that a mesh axis runs over, the one named last changes fastest.
Arguments:
- block_input: bfloat16 [131072, 512], P('dp', 'owner'), may hold values from -6 to 6
- block_middle: bfloat16 [131072, 512], P('dp', 'owner'), may hold values from -6 to 6
- out_grad: bfloat16 [131072, 512], P('dp', 'owner'), may hold values from -0.03125 to 0.03125
- lengths: int32 [256], P('dp'), may hold values from 1 to 512, 98304 in all
- conv_weight: bfloat16 [512, 5, 512], P(None, None, 'owner'), may hold values from -0.125 to 0.125
- block_of_slot: int32 [128], replicated, may hold values from 0 to 39, as said below
- slot_count: int32 [128], P('dp'), may hold values from 0 to 1, as said below
- left_prev: float32 [128, 16384], P('dp'), as said below
- right_prev: float32 [128, 65536], P('dp', 'owner'), as said below
Outputs:
- update: float32 [128, 65536], P('dp', 'owner')
The draws below stay inside these ranges and needn't reach their ends.
Inputs may be any that keep to these rules, and one draw needn't show every extreme that they name: `block_of_slot`: group g owns slots g * 1 to (g + 1) - 1; its first slot_count[g] slots are used. The used slots of all groups name every block exactly once; unused slots hold some block number. `slot_count`: the counts sum to 40. `left_prev`: each 128 x 128 block is symmetric positive definite. `right_prev`: each 128 x 128 block is symmetric positive definite.
All inputs are finite; a program needn't handle non-finite values. No bound on the sum of `lengths` on one device may be relied on, other than what follows from the above.
Results may differ from the reference program's by a relative error of at most 0.01.
Values may be sent and summed in bfloat16 or wider, within the bound.
A program may use at most 64 MiB of HBM per device.

```python
import math
import jax
import jax.numpy as jnp
import numpy as np
from jax import lax

CONV_CHANNELS = 512
KW = 5
FIRST_DILATION1 = 4
SECOND_DILATION2 = 8
BR = 128
LEN = 512
ITERS = 8
NSEQ = 256
TOKENS = 131072
OWNER_CHANNELS = 128
NR = 20
NUNIT = 40
CAP = 1
SLOTS = 128
N_DP = 128
N_OWNER = 4


def owner_table(key):
    unit_key, group_key, slot_key = jax.random.split(key, 3)
    unit_order = jax.random.permutation(unit_key, NUNIT).astype(jnp.int32)
    busiest = jax.random.randint(group_key, (), 0, N_DP)
    chosen = jax.random.permutation(slot_key, (N_DP - 1) * CAP) < NUNIT - CAP
    other_counts = jnp.sum(chosen.astype(jnp.int32).reshape(N_DP - 1, CAP), axis=1)
    groups = jnp.arange(N_DP, dtype=jnp.int32)
    other_index = jnp.clip(groups - (groups > busiest).astype(jnp.int32), 0, N_DP - 2)
    counts = jnp.where(groups == busiest, CAP, other_counts[other_index]).astype(jnp.int32)
    starts = jnp.cumsum(counts) - counts
    ranks = jnp.arange(CAP, dtype=jnp.int32)
    positions = (starts[:, None] + ranks[None, :]) % NUNIT
    return (unit_order[positions].reshape(N_DP * CAP), counts)


def definite_blocks(key, block_count, order_size, low_end, high_end):
    off_key, diag_key = jax.random.split(key)
    raw_values = jax.random.uniform(off_key, (block_count, order_size, order_size), jnp.float32, -1.0, 1.0)
    symmetric = 0.5 * (raw_values + jnp.swapaxes(raw_values, 1, 2))
    identity_mat = jnp.eye(order_size, dtype=jnp.float32)
    coupling = 0.8 * symmetric / order_size
    shape_mat = identity_mat + coupling * (1.0 - identity_mat)
    scales = jnp.exp(jax.random.uniform(diag_key, (block_count, order_size), jnp.float32, math.log(low_end), math.log(high_end)))
    root_scales = jnp.sqrt(scales)
    return shape_mat * root_scales[:, :, None] * root_scales[:, None, :]


def draw_block_of_slot(key, part):
    table, counts = owner_table(key)
    return table


def draw_slot_count(key, part):
    table, counts = owner_table(key)
    return counts


def draw_left_prev(key, part):
    key = jax.random.fold_in(key, 21)
    blocks = definite_blocks(key, SLOTS, BR, 0.001, 10000.0)
    return blocks.reshape(SLOTS, BR * BR)


def draw_right_prev(key, part):
    key = jax.random.fold_in(key, 23)
    blocks = definite_blocks(key, SLOTS * N_OWNER, OWNER_CHANNELS, 0.001, 10000.0)
    return blocks.reshape(SLOTS, N_OWNER * OWNER_CHANNELS * OWNER_CHANNELS)


def level_of(key, extent, shards, low, top_value):
    def one(dim, shards_of):
        draws = jax.random.uniform(jax.random.fold_in(jax.random.fold_in(key, 6), dim), (shards_of,), jnp.float32, low / len(shards), top_value / len(shards))
        return jnp.repeat(jnp.exp(draws), extent[dim] // shards_of).reshape((-1,) + (1,) * (len(extent) - dim - 1))

    loudness = one(*shards[0])
    for cut in shards[1:]:
        loudness = loudness * one(*cut)
    return loudness


def split_up(amount, total, limit, lean):
    weights = [(1 << 20) // math.isqrt(rank ** lean) + 1 for rank in range(2, amount + 1)]
    spare, given = total - limit - (amount - 1), [1] * (amount - 1)
    while spare > 0:
        movable = [i for i in range(amount - 1) if given[i] < limit]
        whole, remaining = sum([weights[i] for i in movable]), spare
        for i in movable:
            addition = min(limit - given[i], max(1, remaining * weights[i] // whole), spare)
            given[i] = given[i] + addition
            spare = spare - addition
    return np.array([limit] + given)


def uneven(key, amount, total, most, slope):
    if amount == 2:
        one = jax.random.randint(key, (), max(1, total - most), min(most, total - 1) + 1)
        return jnp.stack([one, total - one])
    tallies = jnp.asarray(split_up(amount, total, most, slope), jnp.int32)
    twos = (amount - 1) // 2
    source_of, sink = tallies[1:1 + 2 * twos:2], tallies[2:2 + 2 * twos:2]
    room = jnp.minimum(source_of - 1, most - sink)
    shifted = jax.random.randint(jax.random.fold_in(key, 1), (twos,), 0, 1 << 20) % (room + 1)
    tallies = tallies.at[1:1 + 2 * twos:2].set(source_of - shifted).at[2:2 + 2 * twos:2].set(sink + shifted)
    return tallies[jax.random.permutation(jax.random.fold_in(key, 2), amount)]


def normal_values(rng, shape, deviation, limit, pieces=(), kind=jnp.bfloat16):
    values = jax.random.normal(rng, shape, jnp.float32) * deviation
    if len(pieces) > 0:
        values = level_of(rng, shape, pieces, -0.22, 0.18) * values
    return jnp.clip(values, min=-limit, max=limit).astype(kind)


def setup_inputs(seed: int = 0) -> dict:
    splits = jax.random.split(jax.random.key(seed), 10)
    return {
        "block_input": normal_values(splits[0], (TOKENS, CONV_CHANNELS), 1.0, 6.0, ((0, 128), (1, 4))),
        "block_middle": normal_values(splits[1], (TOKENS, CONV_CHANNELS), 1.0, 6.0, ((0, 128), (1, 4))),
        "out_grad": normal_values(splits[2], (TOKENS, CONV_CHANNELS), (2.0 / TOKENS ** 0.5), 0.03125, ((0, 128), (1, 4))),
        "lengths": uneven(splits[3], NSEQ, NSEQ * LEN * 3 // 4, LEN, 0).astype(jnp.int32),
        "conv_weight": normal_values(splits[4], (CONV_CHANNELS, KW, CONV_CHANNELS), (KW * CONV_CHANNELS) ** -0.5, 0.125, ((2, 4),)),
        "block_of_slot": draw_block_of_slot(jax.random.fold_in(splits[9], 71), 0),
        "slot_count": draw_slot_count(jax.random.fold_in(splits[9], 71), 0),
        "left_prev": draw_left_prev(jax.random.fold_in(splits[9], 71), 0),
        "right_prev": draw_right_prev(jax.random.fold_in(splits[9], 71), 0),
    }


decay_rate = 0.9

def shift_rows(values, offset):
    seq_length = values.shape[1]
    margin = abs(offset)
    padded = jnp.pad(values, ((0, 0), (margin, margin), (0, 0)))
    return padded[:, margin + offset:margin + offset + seq_length]

def stacked_taps(gradient, dilation):
    middle = KW // 2
    shifted_list = [shift_rows(gradient, -(tap - middle) * dilation) for tap in range(KW)]
    first_stacked = jnp.concatenate(shifted_list, axis=2)
    return first_stacked.reshape(-1, first_stacked.shape[2])

def kernel_gradient(activations, first_stacked, out_width):
    product = lax.dot_general(activations, first_stacked, (((0,), (0,)), ((), ())), preferred_element_type=jnp.float32)
    return product.reshape(activations.shape[1] * (first_stacked.shape[1] // out_width), out_width)

def gelu_slope(values):
    return 0.5 * (1.0 + lax.erf(values * 0.7071067811865476)) + values * jnp.exp(-0.5 * values * values) * 0.3989422804014327

def batch_product(left, right):
    return jnp.einsum('...ij,...jk->...ik', left, right, precision=lax.Precision.HIGHEST)

def inverse_fourth_root(statistic):
    order_size = statistic.shape[-1]
    identity_mat = jnp.eye(order_size, dtype=jnp.float32)
    frob_norm = jnp.sqrt(lax.optimization_barrier(jnp.sum(statistic * statistic, axis=(-2, -1))))[..., None, None]
    current = statistic / frob_norm
    root_mat = jnp.broadcast_to(identity_mat, statistic.shape)
    for iteration in range(ITERS):
        factor = (5.0 * identity_mat - current) * 0.25
        square = batch_product(factor, factor)
        fourth = batch_product(square, square)
        current = batch_product(fourth, current)
        root_mat = batch_product(root_mat, factor)
    return root_mat * frob_norm ** (-0.25)

def reference(block_input, block_middle, out_grad, lengths, conv_weight, block_of_slot, slot_count, left_prev, right_prev):
    seq_count = lengths.shape[0]
    positions = lax.broadcasted_iota(jnp.int32, (seq_count, LEN), 1)
    valid_mask = (positions < lengths[:, None]).astype(jnp.float32)[:, :, None]

    def activate(values):
        shaped = values.astype(jnp.float32).reshape(seq_count, LEN, CONV_CHANNELS)
        return (jax.nn.gelu(shaped, approximate=False) * valid_mask).astype(jnp.bfloat16).reshape(-1, CONV_CHANNELS)
    first_hidden = activate(block_input)
    second_hidden = activate(block_middle)
    second_gradient = (out_grad.astype(jnp.float32).reshape(seq_count, LEN, CONV_CHANNELS) * valid_mask).astype(jnp.bfloat16)
    second_kernel = kernel_gradient(second_hidden, stacked_taps(second_gradient, SECOND_DILATION2), CONV_CHANNELS)
    back_two = jnp.zeros((seq_count * LEN, CONV_CHANNELS), jnp.float32)
    for weight_piece in range(N_OWNER):
        first_stacked = stacked_taps(second_gradient[:, :, weight_piece * OWNER_CHANNELS:(weight_piece + 1) * OWNER_CHANNELS], SECOND_DILATION2)
        flat_weight = conv_weight[:, :, weight_piece * OWNER_CHANNELS:(weight_piece + 1) * OWNER_CHANNELS].reshape(CONV_CHANNELS, KW * OWNER_CHANNELS)
        partial_value = lax.dot_general(first_stacked, flat_weight, (((1,), (1,)), ((), ())), preferred_element_type=jnp.float32)
        rounded = lax.optimization_barrier(partial_value.astype(jnp.bfloat16))
        back_two = back_two + rounded.astype(jnp.float32)
    slope_vals = gelu_slope(block_middle.astype(jnp.float32).reshape(seq_count, LEN, CONV_CHANNELS))
    first_gradient = (second_gradient.astype(jnp.float32) + slope_vals * valid_mask * back_two.reshape(seq_count, LEN, CONV_CHANNELS)).astype(jnp.bfloat16)
    first_kernel = kernel_gradient(first_hidden, stacked_taps(first_gradient, FIRST_DILATION1), CONV_CHANNELS)
    kernels = jnp.stack([first_kernel, second_kernel])
    tiles_all = kernels.reshape(2, NR, BR, N_OWNER, OWNER_CHANNELS).transpose(0, 1, 3, 2, 4).reshape(-1, N_OWNER, BR, OWNER_CHANNELS)
    slot_tiles = tiles_all[block_of_slot]
    highest = lax.Precision.HIGHEST
    left_part = jnp.einsum('spab,spcb->sac', slot_tiles, slot_tiles, precision=highest)
    right_part = jnp.einsum('spab,spac->spbc', slot_tiles, slot_tiles, precision=highest)
    left_stat = decay_rate * left_prev.reshape(SLOTS, BR, BR) + (1.0 - decay_rate) * left_part
    right_stat = decay_rate * right_prev.reshape(SLOTS, N_OWNER, OWNER_CHANNELS, OWNER_CHANNELS) + (1.0 - decay_rate) * right_part
    left_root = inverse_fourth_root(left_stat)
    right_root = inverse_fourth_root(right_stat)
    mixed = jnp.einsum('sab,spbc->spac', left_root, slot_tiles, precision=highest) + jnp.einsum('spab,spbc->spac', slot_tiles, right_root, precision=highest)
    raw_update = jnp.einsum('sab,spbc->spac', left_root, mixed, precision=highest) + jnp.einsum('spab,spbc->spac', mixed, right_root, precision=highest)
    squares = lax.optimization_barrier(jnp.sum(raw_update * raw_update, axis=(1, 2, 3)))
    inverse_rms = 1.0 / jnp.sqrt(squares / (N_OWNER * BR * OWNER_CHANNELS) + 1e-06)
    live_slots = jnp.arange(SLOTS, dtype=jnp.int32) % CAP < jnp.repeat(slot_count, CAP)
    result = jnp.where(live_slots[:, None, None, None], raw_update * inverse_rms[:, None, None, None], 0.0)
    return result.reshape(SLOTS, N_OWNER * BR * OWNER_CHANNELS)
```

```python
import jax
import jax.numpy as jnp
from jax import lax
from jax.experimental import pallas as pl
from jax.experimental.pallas import tpu as pltpu
from jax.sharding import PartitionSpec as P

MESH = pl.DeviceIdType.MESH
F32, BF16 = jnp.float32, jnp.bfloat16
KW = 5
BR = 128
LEN = 512
PAD = 16
NS = 2
NX, NY, NZ = 4, 8, 8
ITERS = 8
DECAY = 0.9
HIGH = lax.Precision.HIGHEST


def mm(a, b):
    return jnp.dot(a, b, precision=HIGH, preferred_element_type=F32)


def inverse_fourth_roots(stats):
    rows = lax.broadcasted_iota(jnp.int32, (BR, BR), 0)
    cols = lax.broadcasted_iota(jnp.int32, (BR, BR), 1)
    eye = (rows == cols).astype(F32)
    norms = [jnp.sqrt(jnp.sum(s * s, axis=(0, 1), keepdims=True)) for s in stats]
    cur = [s / n for s, n in zip(stats, norms)]
    root = None
    for it in range(ITERS):
        fac = [(5.0 * eye - m) * 0.25 for m in cur]
        root = fac if it == 0 else [mm(r, f) for r, f in zip(root, fac)]
        if it < ITERS - 1:
            square = [mm(f, f) for f in fac]
            fourth = [mm(s, s) for s in square]
            cur = [mm(f, m) for f, m in zip(fourth, cur)]
    scale = [1.0 / jnp.sqrt(jnp.sqrt(n)) for n in norms]
    return [r * s for r, s in zip(root, scale)]


def peer_at(major, minor, core):
    z = major + core * (minor - major)
    y = minor + core * (major - minor)
    return (z * NY + y) * 2 + core


def kernel(
    x1_ref, x2_ref, g_ref, len_ref, w_ref, bos_ref, cnt_ref, lprev_ref, rprev_ref, out_ref,
    gbuf, hbuf, h2t, slope, wbuf, gst, g1, back, kbuf,
    c0, p1, r1, u1, p2, r2, p3, r3, rows_ref, d3, e3, d4, f4, tile_ref, lp, lr, sq, sr,
    gs_sem, gr_sem, hs_sem, hr_sem, ws_sem, wr_sem, c0_sem, s1_sem, r1_sem, s2_sem, r2_sem,
    s3_sem, r3_sem, ds_sem, dr_sem, fs_sem, fr_sem, ls_sem, lr_sem, qs_sem, qr_sem,
):
    dp, p = lax.axis_index("dp"), lax.axis_index("owner")
    c = dp % 2
    y = (dp // 2) % NY
    z = dp // (2 * NY)
    a = z + c * (y - z)
    b = y + c * (z - y)
    right, left = (p + 1) % NX, (p + 3) % NX

    def rcopy(src, dst, ss, rs, dev):
        return pltpu.make_async_remote_copy(
            src_ref=src, dst_ref=dst, send_sem=ss, recv_sem=rs, device_id=dev, device_id_type=MESH
        )

    barrier = pltpu.get_barrier_semaphore()

    def greet(dev):
        pl.semaphore_signal(barrier, inc=1, device_id=dev, device_id_type=MESH)

    @pl.loop(1, NX)
    def _(i):
        greet((dp, (p + i) % NX))

    @pl.loop(1, 2 * NZ)
    def _(i):
        k = (z * 2 + c + i) % (2 * NZ)
        greet((((k // 2) * NY + y) * 2 + k % 2, p))

    @pl.loop(0, 2 * (NY - 1))
    def _(i):
        greet(((z * NY + (y + 1 + i // 2) % NY) * 2 + i % 2, p))

    zpad = jnp.zeros((PAD, BR), BF16)
    for slot in range(NX):
        for s in range(NS):
            gbuf[slot, s, 0:PAD, :] = zpad
            gbuf[slot, s, PAD + LEN : PAD + LEN + PAD, :] = zpad
    for s in range(NS):
        g1[s, 0:PAD, :] = zpad
        g1[s, PAD + LEN : PAD + LEN + PAD, :] = zpad
    tok = lax.broadcasted_iota(jnp.int32, (LEN, BR), 0)
    for s in range(NS):
        v = g_ref[s * LEN : (s + 1) * LEN, :].astype(F32)
        gbuf[0, s, PAD : PAD + LEN, :] = jnp.where(tok < len_ref[s], v, 0.0).astype(BF16)

    pl.semaphore_wait(barrier, 3 + 15 + 14)

    def gpiece(slot, s):
        return gbuf.at[slot, s, pl.ds(PAD, LEN), :]

    def hpiece(slot, s):
        return hbuf.at[slot, s]

    plan = [
        (0, 3, 1, right), (0, 3, 0, right), (0, 1, 0, left), (0, 1, 1, left),
        (1, 2, 0, left), (3, 2, 1, right),
    ]

    def xcopy(piece, ss, rs, i):
        src, dst, s, dev = plan[i]
        return rcopy(piece(src, s), piece(dst, s), ss.at[i], rs.at[i], (dp, dev))

    def xland(piece, ss, rs, i):
        src, dst, s, dev = plan[i]
        rcopy(piece(dst, s), piece(dst, s), ss.at[i], rs.at[i], (dp, dev)).wait_recv()

    for i in (0, 2, 1, 3):
        xcopy(gpiece, gs_sem, gr_sem, i).start()

    def wcopy(i):
        q = (p + i) % NX
        src = w_ref.at[:, pl.ds(pl.multiple_of(q * BR, BR), BR), :]
        return rcopy(src, wbuf.at[NX - i], ws_sem.at[NX - i], wr_sem.at[NX - i], (dp, q))

    for i in range(1, NX):
        wcopy(i).start()
    wbuf[0] = w_ref[:, pl.ds(pl.multiple_of(p * BR, BR), BR), :]

    @pl.loop(0, NS * LEN // BR)
    def _(i):
        s = i // (LEN // BR)
        t0 = pl.multiple_of((i % (LEN // BR)) * BR, BR)
        r0 = pl.multiple_of(i * BR, BR)
        valid = (lax.broadcasted_iota(jnp.int32, (BR, BR), 0) + t0 < len_ref[s]).astype(F32)
        x = x1_ref[pl.ds(r0, BR), :].astype(F32)
        h = x * (0.5 * (1.0 + lax.erf(x * 0.7071067811865476))) * valid
        hbuf[0, s, :, pl.ds(t0, BR)] = h.T.astype(BF16)
        x = x2_ref[pl.ds(r0, BR), :].astype(F32)
        phi = 0.5 * (1.0 + lax.erf(x * 0.7071067811865476))
        h2t[s, :, pl.ds(t0, BR)] = (x * phi * valid).T.astype(BF16)
        slope[pl.ds(r0, BR), :] = (phi + x * jnp.exp(-0.5 * x * x) * 0.3989422804014327) * valid

    xland(gpiece, gs_sem, gr_sem, 0)
    xcopy(gpiece, gs_sem, gr_sem, 5).start()
    xland(gpiece, gs_sem, gr_sem, 2)
    xcopy(gpiece, gs_sem, gr_sem, 4).start()
    for i in (0, 2, 1, 3):
        xcopy(hpiece, hs_sem, hr_sem, i).start()

    def stack(src, dilation):
        for s in range(NS):
            for k in range(KW):
                r0 = PAD - (k - KW // 2) * dilation
                gst[s, :, k * BR : (k + 1) * BR] = src[s, r0 : r0 + LEN, :]

    def put_rows(kk, slot, prod):
        for k in range(KW):
            kbuf[kk, slot, pl.ds(k, BR, stride=KW), :] = prod[:, k * BR : (k + 1) * BR]

    def second_piece(slot):
        stack(gbuf.at[slot], 8)
        prod = jnp.dot(h2t[0], gst[0], preferred_element_type=F32)
        prod += jnp.dot(h2t[1], gst[1], preferred_element_type=F32)
        put_rows(1, slot, prod)
        wcat = jnp.concatenate([wbuf[slot, k] for k in range(KW)], axis=1)
        for s in range(NS):
            part = lax.dot_general(gst[s], wcat, (((1,), (1,)), ((), ())), preferred_element_type=F32)
            if slot == 0:
                back[s] = part
            else:
                back[s] += part

    def wland(i):
        wcopy(NX - i).wait_recv()

    second_piece(0)
    xland(gpiece, gs_sem, gr_sem, 1)
    wland(3)
    second_piece(3)
    xland(gpiece, gs_sem, gr_sem, 3)
    wland(1)
    second_piece(1)
    xland(gpiece, gs_sem, gr_sem, 4)
    xland(gpiece, gs_sem, gr_sem, 5)
    wland(2)
    second_piece(2)

    sib = dp + 1 - 2 * c
    NT = NX * KW

    def core_copy(kk):
        other = pl.ds(pl.multiple_of((1 - c) * 64, 64), 64)
        return rcopy(
            ktile(kk).at[:, other, :], c0.at[kk], c0_sem.at[2 * kk], c0_sem.at[2 * kk + 1], (sib, p)
        )

    def ktile(kk):
        return kbuf.at[kk].reshape(NT, BR, BR)

    def major_copy(kk, t, land):
        return rcopy(
            r1.at[kk, t] if land else p1.at[kk, t], r1.at[kk, t if land else a],
            s1_sem.at[kk, t], r1_sem.at[kk, t if land else a], (peer_at(t, b, c), p),
        )

    def minor_copy(kk, t, land):
        return rcopy(
            r2.at[kk, t] if land else p2.at[kk, t], r2.at[kk, t if land else b],
            s2_sem.at[kk, t], r2_sem.at[kk, t if land else b], (peer_at(a, t, c), p),
        )

    def to_major(kk):
        core_copy(kk).wait_recv()
        mine = pl.multiple_of(c * 64, 64)

        @pl.loop(0, 8)
        def _(t):
            t8 = pl.multiple_of(t * 8, 8)
            own = ktile(kk)[:, pl.ds(mine + t8, 8), :]
            p1[kk, t] = (own + c0[kk, :, pl.ds(t8, 8), :]).reshape(NT * 8, BR).astype(BF16)

        @pl.loop(1, 8)
        def _(i):
            major_copy(kk, (a + i) % 8, False).start()

    def to_minor(kk):
        u1[kk] = p1[kk, a].astype(F32)

        @pl.loop(1, 8)
        def _(i):
            t = (a + i) % 8
            major_copy(kk, t, True).wait_recv()
            u1[kk] += r1[kk, t].astype(F32)

        for t in range(8):
            p2[kk, t, 0:NT, :] = u1[kk, pl.ds(t, NT, stride=8), :]

        @pl.loop(1, 8)
        def _(i):
            minor_copy(kk, (b + i) % 8, False).start()

    def minor_sum(kk):
        acc = p2[kk, b, 0:NT, :]
        for i in range(1, 8):
            t = (b + i) % 8
            minor_copy(kk, t, True).wait_recv()
            acc = acc + r2[kk, t, 0:NT, :]
        return acc

    core_copy(1).start()

    for s in range(NS):
        g1[s, PAD : PAD + LEN, :] = (
            gbuf[0, s, PAD : PAD + LEN, :].astype(F32) + slope[s * LEN : (s + 1) * LEN, :] * back[s]
        ).astype(BF16)
    to_major(1)
    stack(g1, 4)

    def first_piece(slot):
        prod = jnp.dot(hbuf[slot, 0], gst[0], preferred_element_type=F32)
        prod += jnp.dot(hbuf[slot, 1], gst[1], preferred_element_type=F32)
        put_rows(0, slot, prod)

    first_piece(0)
    xland(hpiece, hs_sem, hr_sem, 0)
    xcopy(hpiece, hs_sem, hr_sem, 5).start()
    xland(hpiece, hs_sem, hr_sem, 2)
    xcopy(hpiece, hs_sem, hr_sem, 4).start()
    xland(hpiece, hs_sem, hr_sem, 1)
    first_piece(3)
    xland(hpiece, hs_sem, hr_sem, 3)
    first_piece(1)
    to_minor(1)
    xland(hpiece, hs_sem, hr_sem, 4)
    xland(hpiece, hs_sem, hr_sem, 5)
    first_piece(2)
    core_copy(0).start()

    acc = minor_sum(1)
    for slot in range(NX):
        p3[slot, 0:KW, :] = acc[slot * KW : (slot + 1) * KW, :]

    def piece_copy(i, land):
        q = (p + i) % NX
        return rcopy(
            r3.at[q] if land else p3.at[i], r3.at[q if land else p],
            s3_sem.at[i], r3_sem.at[q if land else p], (dp, q),
        )

    for i in range(1, NX):
        piece_copy(i, False).start()
    to_major(0)
    for i in range(1, NX):
        piece_copy(i, True).wait_recv()
        q = (p + i) % NX
        rows_ref[pl.ds(pl.multiple_of(32 + q * 8, 8), 8), :] = r3[q]
    rows_ref[pl.ds(pl.multiple_of(32 + p * 8, 8), 8), :] = p3[0]
    to_minor(0)
    acc = minor_sum(0)
    for slot in range(NX):
        q = (p + slot) % NX
        rows_ref[pl.ds(pl.multiple_of(q * 8, 8), KW), :] = acc[slot * KW : (slot + 1) * KW, :]

    @pl.loop(0, 8)
    def _(t):
        for m in range(8):
            for core in range(2):
                zz = t + c * (m - t)
                yy = m + c * (t - m)
                u = bos_ref[(zz * NY + yy) * 2 + core]
                second = (u >= 20).astype(jnp.int32)
                r = u - 20 * second
                row = second * 32 + (r // 5) * 8 + r % 5
                d3[t, pl.ds(m * 2 + core, 1), :] = rows_ref[pl.ds(row, 1), :]

    def slot_copy(t, land):
        return rcopy(
            e3.at[t] if land else d3.at[t], e3.at[t if land else a],
            ds_sem.at[t], dr_sem.at[t if land else a], (peer_at(t, b, c), p),
        )

    @pl.loop(1, 8)
    def _(i):
        slot_copy((a + i) % 8, False).start()

    e3[a] = d3[a]

    @pl.loop(1, 8)
    def _(i):
        slot_copy((a + i) % 8, True).wait_recv()

    for i in range(16):
        d4[i] = e3[:, i, :]

    def group_copy(i):
        m, core = i // 2, i % 2
        zz = a + c * (m - a)
        yy = m + c * (a - m)
        me = c * 8 + b
        return rcopy(
            d4.at[i], f4.at[me], fs_sem.at[i], fr_sem.at[me], ((zz * NY + yy) * 2 + core, p)
        )

    def group_land(i):
        rcopy(f4.at[i], f4.at[i], fs_sem.at[i], fr_sem.at[i], (sib, p)).wait_recv()

    @pl.loop(1, 16)
    def _(i):
        group_copy((b * 2 + c + i) % 16).start()

    f4[c * 8 + b] = d4[b * 2 + c]

    @pl.loop(1, 16)
    def _(i):
        group_land((c * 8 + b + i) % 16)

    for core in range(2):
        for t in range(8):
            tile_ref[core * 64 + t * 8 : core * 64 + t * 8 + 8, :] = f4[core * 8 : core * 8 + 8, t, :]

    tile = tile_ref[...]
    tile_t = tile.T
    lp[...] = mm(tile, tile_t).astype(BF16)

    def left_copy(i, land):
        q = (p + i) % NX
        return rcopy(
            lr.at[q] if land else lp, lr.at[q if land else p],
            ls_sem.at[i], lr_sem.at[q if land else p], (dp, q),
        )

    for i in range(1, NX):
        left_copy(i, False).start()
    right_stat = DECAY * rprev_ref[...] + (1.0 - DECAY) * mm(tile_t, tile)
    left_sum = lp[...].astype(F32)
    for i in range(1, NX):
        left_copy(i, True).wait_recv()
        left_sum = left_sum + lr[(p + i) % NX].astype(F32)
    left_stat = DECAY * lprev_ref[...] + (1.0 - DECAY) * left_sum
    left_root, right_root = inverse_fourth_roots([left_stat, right_stat])
    mixed = mm(left_root, tile) + mm(tile, right_root)
    raw = mm(left_root, mixed) + mm(mixed, right_root)

    sq[...] = jnp.broadcast_to(jnp.sum(raw * raw, axis=(0, 1), keepdims=True), (8, BR))

    def square_copy(i, land):
        q = (p + i) % NX
        return rcopy(
            sr.at[q] if land else sq, sr.at[q if land else p],
            qs_sem.at[i], qr_sem.at[q if land else p], (dp, q),
        )

    for i in range(1, NX):
        square_copy(i, False).start()
    total = sq[...]
    for i in range(1, NX):
        square_copy(i, True).wait_recv()
        total = total + sr[(p + i) % NX]
    inv = 1.0 / jnp.sqrt(total[0:1, 0:1] / (NX * BR * BR) + 1e-6)
    out_ref[...] = jnp.where(cnt_ref[0] > 0, raw * inv, 0.0)

    for i in range(6):
        xcopy(gpiece, gs_sem, gr_sem, i).wait_send()
        xcopy(hpiece, hs_sem, hr_sem, i).wait_send()
    for i in range(1, NX):
        wcopy(i).wait_send()
        piece_copy(i, False).wait_send()
        left_copy(i, False).wait_send()
        square_copy(i, False).wait_send()
    for kk in range(2):
        core_copy(kk).wait_send()

    @pl.loop(1, 8)
    def _(i):
        ta, tb = (a + i) % 8, (b + i) % 8
        for kk in range(2):
            major_copy(kk, ta, False).wait_send()
            minor_copy(kk, tb, False).wait_send()
        slot_copy(ta, False).wait_send()

    @pl.loop(1, 16)
    def _(i):
        group_copy((b * 2 + c + i) % 16).wait_send()


def local(
    block_input, block_middle, out_grad, lengths, conv_weight, block_of_slot, slot_count, left_prev, right_prev
):
    vmem = pl.BlockSpec(memory_space=pltpu.VMEM)
    smem = pl.BlockSpec(memory_space=pltpu.SMEM)
    dma = pltpu.SemaphoreType.DMA
    NT = NX * KW
    out = pl.pallas_call(
        kernel,
        out_shape=jax.ShapeDtypeStruct((BR, BR), F32),
        in_specs=[vmem, vmem, vmem, smem, vmem, smem, smem, vmem, vmem],
        out_specs=vmem,
        scratch_shapes=[
            pltpu.VMEM((NX, NS, LEN + 2 * PAD, BR), BF16),
            pltpu.VMEM((NX, NS, BR, LEN), BF16),
            pltpu.VMEM((NS, BR, LEN), BF16),
            pltpu.VMEM((NS * LEN, BR), F32),
            pltpu.VMEM((NX, KW, BR, BR), BF16),
            pltpu.VMEM((NS, LEN, KW * BR), BF16),
            pltpu.VMEM((NS, LEN + 2 * PAD, BR), BF16),
            pltpu.VMEM((NS, LEN, BR), F32),
            pltpu.VMEM((2, NX, KW * BR, BR), F32),
            pltpu.VMEM((2, NT, 64, BR), F32),
            pltpu.VMEM((2, 8, NT * 8, BR), BF16),
            pltpu.VMEM((2, 8, NT * 8, BR), BF16),
            pltpu.VMEM((2, NT * 8, BR), F32),
            pltpu.VMEM((2, 8, 24, BR), F32),
            pltpu.VMEM((2, 8, 24, BR), F32),
            pltpu.VMEM((NX, 8, BR), F32),
            pltpu.VMEM((NX, 8, BR), F32),
            pltpu.VMEM((64, BR), F32),
            pltpu.VMEM((8, 16, BR), F32),
            pltpu.VMEM((8, 16, BR), F32),
            pltpu.VMEM((16, 8, BR), F32),
            pltpu.VMEM((16, 8, BR), F32),
            pltpu.VMEM((BR, BR), F32),
            pltpu.VMEM((BR, BR), BF16),
            pltpu.VMEM((NX, BR, BR), BF16),
            pltpu.VMEM((8, BR), F32),
            pltpu.VMEM((NX, 8, BR), F32),
            dma((6,)), dma((6,)), dma((6,)), dma((6,)), dma((NX,)), dma((NX,)), dma((4,)),
            dma((2, 8)), dma((2, 8)), dma((2, 8)), dma((2, 8)), dma((NX,)), dma((NX,)),
            dma((8,)), dma((8,)), dma((16,)), dma((16,)), dma((NX,)), dma((NX,)), dma((NX,)), dma((NX,)),
        ],
        compiler_params=pltpu.CompilerParams(
            collective_id=0, has_side_effects=True, vmem_limit_bytes=40 * 1024 * 1024
        ),
    )(
        block_input, block_middle, out_grad, lengths, conv_weight.transpose(1, 0, 2), block_of_slot,
        slot_count, left_prev.reshape(BR, BR), right_prev.reshape(BR, BR),
    )
    return out.reshape(1, BR * BR)


def solution(mesh):
    return jax.shard_map(
        local,
        mesh=mesh,
        in_specs=(
            P("dp", "owner"), P("dp", "owner"), P("dp", "owner"), P("dp"), P(None, None, "owner"), P(),
            P("dp"), P("dp", None), P("dp", "owner"),
        ),
        out_specs=P("dp", "owner"),
        check_vma=False,
    )
```

```python
import jax
import jax.numpy as jnp
from jax import lax
from jax.experimental import pallas as pl
from jax.experimental.pallas import tpu as pltpu
from jax.sharding import PartitionSpec as P

MESH = pl.DeviceIdType.MESH
F32, BF16 = jnp.float32, jnp.bfloat16
KW = 5
BR = 128
LEN = 512
PAD = 16
NS = 2
NX, NY, NZ = 4, 8, 8
ITERS = 8
DECAY = 0.9


def split(a):
    high = a.astype(BF16)
    return high, (a - high.astype(F32)).astype(BF16)


def mm(a, b):
    (ah, al), (bh, bl) = a, b
    left = jnp.concatenate([ah, al], axis=1)
    right = jnp.concatenate(
        [jnp.concatenate([bh, bl], axis=1), jnp.concatenate([bh, jnp.zeros_like(bl)], axis=1)], axis=0
    )
    both = jnp.dot(left, right, preferred_element_type=F32)
    return both[:, :BR] + both[:, BR:]


def inverse_fourth_roots(stats):
    rows = lax.broadcasted_iota(jnp.int32, (BR, BR), 0)
    cols = lax.broadcasted_iota(jnp.int32, (BR, BR), 1)
    eye = (rows == cols).astype(F32)
    norms = [jnp.sqrt(jnp.sum(s * s, axis=(0, 1), keepdims=True)) for s in stats]
    cur = [s / n for s, n in zip(stats, norms)]
    root = None
    for it in range(ITERS):
        fac = [1.25 * eye - 0.25 * m for m in cur]
        parts = [split(f) for f in fac]
        if it < ITERS - 1:
            square = [split(mm(f, f)) for f in parts]
            fourth = [split(mm(s, s)) for s in square]
            cur = [mm(f, split(m)) for f, m in zip(fourth, cur)]
        root = fac if it == 0 else [mm(split(r), f) for r, f in zip(root, parts)]
    scale = [1.0 / jnp.sqrt(jnp.sqrt(n)) for n in norms]
    return [r * s for r, s in zip(root, scale)]


def peer_at(major, minor, core):
    z = major + core * (minor - major)
    y = minor + core * (major - minor)
    return (z * NY + y) * 2 + core


PLACES = (0, 3, 1, 2)
UNITS = ((1, 0, 4), (0, 0, 3), (0, 3, 1))


def padded_rows(places):
    return -(-places * KW * 8 // 16) * 16


def kernel(
    x1_hbm, x2_hbm, g_hbm, len_ref, w_ref, bos_ref, cnt_ref, lprev_hbm, rprev_hbm, out_ref,
    x1_ref, x2_ref, g_ref, lprev_ref, rprev,
    gbuf, hbuf, h2t, slope, wbuf, gst, g1, kbuf,
    c0, c1, c2, pa0, pa1, pa2, ra0, ra1, ra2, pb0, pb1, pb2, rb0, rb1, rb2, p3, r3, rows_ref, d4, f4, tiles,
    gs_sem, gr_sem, hs_sem, hr_sem, ws_sem, wr_sem, as_sem, ar_sem, c0_sem, s1_sem, r1_sem, s2_sem, r2_sem,
    s3_sem, r3_sem, fs_sem, fr_sem, vs_sem, vr_sem, ts_sem, tr_sem, in_sem,
):
    dp, p = lax.axis_index("dp"), lax.axis_index("owner")
    c = dp % 2
    y = (dp // 2) % NY
    z = dp // (2 * NY)
    a = z + c * (y - z)
    b = y + c * (z - y)
    right, left = (p + 1) % NX, (p + 3) % NX
    core_in, pa, ra = (c0, c1, c2), (pa0, pa1, pa2), (ra0, ra1, ra2)
    pb, rb = (pb0, pb1, pb2), (rb0, rb1, rb2)

    def rcopy(src, dst, ss, rs, dev):
        return pltpu.make_async_remote_copy(
            src_ref=src, dst_ref=dst, send_sem=ss, recv_sem=rs, device_id=dev, device_id_type=MESH
        )

    def fetch(i, src, dst):
        return pltpu.make_async_copy(src, dst, in_sem.at[i])

    own = pl.ds(pl.multiple_of(p * BR, BR), BR)
    fetches = [
        fetch(0, g_hbm, g_ref), fetch(1, x1_hbm, x1_ref), fetch(2, x2_hbm, x2_ref),
        fetch(3, w_ref.at[:, own, :], wbuf.at[0]), fetch(4, lprev_hbm, lprev_ref), fetch(5, rprev_hbm, rprev.at[0]),
    ]
    for f in fetches:
        f.start()

    sent, loops = [], []

    def send(copy):
        copy.start()
        sent.append(copy)

    def drain():
        for copy in sent:
            copy.wait_send()
        for count, copy in loops:

            @pl.loop(1, count)
            def _(i):
                copy(i).wait_send()

    barrier = pltpu.get_barrier_semaphore()

    def greet(dev):
        pl.semaphore_signal(barrier, inc=1, device_id=dev, device_id_type=MESH)

    @pl.loop(1, NX)
    def _(i):
        greet((dp, (p + i) % NX))

    @pl.loop(1, 2 * NZ)
    def _(i):
        k = (z * 2 + c + i) % (2 * NZ)
        greet((((k // 2) * NY + y) * 2 + k % 2, p))

    @pl.loop(0, 2 * (NY - 1))
    def _(i):
        greet(((z * NY + (y + 1 + i // 2) % NY) * 2 + i % 2, p))

    zpad = jnp.zeros((PAD, BR), BF16)
    for slot in range(NX):
        for s in range(NS):
            gbuf[slot, s, 0:PAD, :] = zpad
            gbuf[slot, s, PAD + LEN : PAD + LEN + PAD, :] = zpad
    for s in range(NS):
        g1[s, 0:PAD, :] = zpad
        g1[s, PAD + LEN : PAD + LEN + PAD, :] = zpad
    tok = lax.broadcasted_iota(jnp.int32, (LEN, BR), 0)
    fetches[0].wait()
    for s in range(NS):
        v = g_ref[s * LEN : (s + 1) * LEN, :].astype(F32)
        gbuf[0, s, PAD : PAD + LEN, :] = jnp.where(tok < len_ref[s], v, 0.0).astype(BF16)

    pl.semaphore_wait(barrier, 3 + 15 + 14)

    def gpiece(slot, s):
        return gbuf.at[slot, s, pl.ds(PAD, LEN), :]

    def hpiece(slot, s):
        return hbuf.at[slot, s]

    plan = [
        (0, 3, 1, right), (0, 3, 0, right), (0, 1, 0, left), (0, 1, 1, left),
        (1, 2, 0, left), (3, 2, 1, right),
    ]

    def xcopy(piece, ss, rs, i):
        src, dst, s, dev = plan[i]
        return rcopy(piece(src, s), piece(dst, s), ss.at[i], rs.at[i], (dp, dev))

    def xland(piece, ss, rs, i):
        src, dst, s, dev = plan[i]
        rcopy(piece(dst, s), piece(dst, s), ss.at[i], rs.at[i], (dp, dev)).wait_recv()

    def wcopy(i):
        q = (p + i) % NX
        src = w_ref.at[:, pl.ds(pl.multiple_of(q * BR + a * 16, 16), 16), :]
        dst = wbuf.at[NX - i, :, pl.ds(pl.multiple_of(a * 16, 16), 16), :]
        return rcopy(src, dst, ws_sem.at[NX - i], wr_sem.at[NX - i], (dp, q))

    def wpart(t):
        return wbuf.at[pl.ds(1, NX - 1), :, pl.ds(pl.multiple_of(t * 16, 16), 16), :]

    def wspread(i):
        t = (a + i) % 8
        return rcopy(wpart(a), wpart(a), as_sem.at[t], ar_sem.at[a], (peer_at(t, b, c), p))

    def wspread_land(i):
        t = (a + i) % 8
        rcopy(wpart(t), wpart(t), as_sem.at[t], ar_sem.at[t], (peer_at(t, b, c), p)).wait_recv()

    for i in range(1, NX):
        send(wcopy(i))
    for i in (0, 2, 1, 3):
        send(xcopy(gpiece, gs_sem, gr_sem, i))

    fetches[1].wait()

    @pl.loop(0, NS * LEN // BR)
    def _(i):
        s = i // (LEN // BR)
        t0 = pl.multiple_of((i % (LEN // BR)) * BR, BR)
        r0 = pl.multiple_of(i * BR, BR)
        valid = (lax.broadcasted_iota(jnp.int32, (BR, BR), 0) + t0 < len_ref[s]).astype(F32)
        x = x1_ref[pl.ds(r0, BR), :].astype(F32)
        h = x * (0.5 * (1.0 + lax.erf(x * 0.7071067811865476))) * valid
        hbuf[0, s, :, pl.ds(t0, BR)] = h.T.astype(BF16)

    for i in range(1, NX):
        wcopy(i).wait_recv()

    @pl.loop(1, 8)
    def _(i):
        wspread(i).start()

    loops.append((8, wspread))
    fetches[2].wait()

    @pl.loop(0, NS * LEN // BR)
    def _(i):
        s = i // (LEN // BR)
        t0 = pl.multiple_of((i % (LEN // BR)) * BR, BR)
        r0 = pl.multiple_of(i * BR, BR)
        valid = (lax.broadcasted_iota(jnp.int32, (BR, BR), 0) + t0 < len_ref[s]).astype(F32)
        x = x2_ref[pl.ds(r0, BR), :].astype(F32)
        phi = 0.5 * (1.0 + lax.erf(x * 0.7071067811865476))
        h2t[s, :, pl.ds(t0, BR)] = (x * phi * valid).T.astype(BF16)
        slope[pl.ds(r0, BR), :] = (phi + x * jnp.exp(-0.5 * x * x) * 0.3989422804014327) * valid

    xland(gpiece, gs_sem, gr_sem, 0)
    send(xcopy(gpiece, gs_sem, gr_sem, 5))
    xland(gpiece, gs_sem, gr_sem, 2)
    send(xcopy(gpiece, gs_sem, gr_sem, 4))

    def stack(src, slot, dilation):
        for s in range(NS):
            for k in range(KW):
                r0 = PAD - (k - KW // 2) * dilation
                gst[slot, s, :, k * BR : (k + 1) * BR] = src[s, r0 : r0 + LEN, :]

    def put_piece(kk, place, acts, slot):
        prod = jnp.dot(acts[0], gst[slot, 0], preferred_element_type=F32)
        prod += jnp.dot(acts[1], gst[slot, 1], preferred_element_type=F32)
        for k in range(KW):
            kbuf[kk, place, pl.ds(k, BR, stride=KW), :] = prod[:, k * BR : (k + 1) * BR]

    def second_piece(place):
        stack(gbuf.at[PLACES[place]], PLACES[place], 8)
        put_piece(1, place, h2t, PLACES[place])

    second_piece(0)
    xland(gpiece, gs_sem, gr_sem, 1)
    second_piece(1)
    xland(gpiece, gs_sem, gr_sem, 3)
    for i in (0, 2, 1, 3):
        send(xcopy(hpiece, hs_sem, hr_sem, i))
    second_piece(2)
    xland(gpiece, gs_sem, gr_sem, 4)
    xland(gpiece, gs_sem, gr_sem, 5)
    second_piece(3)

    sib = dp + 1 - 2 * c

    def ktile(u):
        kk, first, places = UNITS[u]
        return kbuf.at[kk].reshape(NX * KW, BR, BR).at[pl.ds(first * KW, places * KW)]

    def core_copy(u):
        other = pl.ds(pl.multiple_of((1 - c) * 64, 64), 64)
        return rcopy(
            ktile(u).at[:, other, :], core_in[u], c0_sem.at[2 * u], c0_sem.at[2 * u + 1], (sib, p)
        )

    def major_copy(u, t, land):
        return rcopy(
            ra[u].at[t] if land else pa[u].at[t], ra[u].at[t if land else a],
            s1_sem.at[u, t], r1_sem.at[u, t if land else a], (peer_at(t, b, c), p),
        )

    def minor_copy(u, t, land):
        return rcopy(
            rb[u].at[t] if land else pb[u], rb[u].at[t if land else b],
            s2_sem.at[u, t], r2_sem.at[u, t if land else b], (peer_at(a, t, c), p),
        )

    def to_major(u):
        core_copy(u).wait_recv()
        rows = UNITS[u][2] * KW * 8
        mine = pl.multiple_of(c * 64, 64)

        @pl.loop(0, 8)
        def _(t):
            t8 = pl.multiple_of(t * 8, 8)
            both = ktile(u)[:, pl.ds(mine + t8, 8), :] + core_in[u][:, pl.ds(t8, 8), :]
            both = both.reshape(rows, BR)
            if padded_rows(UNITS[u][2]) > rows:
                both = jnp.concatenate([both, jnp.zeros((8, BR), F32)], axis=0)
            pa[u][t] = both.astype(BF16)

        @pl.loop(1, 8)
        def _(i):
            major_copy(u, (a + i) % 8, False).start()

        loops.append((8, lambda i: major_copy(u, (a + i) % 8, False)))

    def to_minor(u):
        acc = pa[u][a].astype(F32)
        for i in range(1, 8):
            t = (a + i) % 8
            major_copy(u, t, True).wait_recv()
            acc = acc + ra[u][t].astype(F32)
        pb[u][...] = acc.astype(BF16)

        @pl.loop(1, 8)
        def _(i):
            minor_copy(u, (b + i) % 8, False).start()

        loops.append((8, lambda i: minor_copy(u, (b + i) % 8, False)))

    def minor_sum(u):
        acc = pb[u][...].astype(F32)
        for i in range(1, 8):
            t = (b + i) % 8
            minor_copy(u, t, True).wait_recv()
            acc = acc + rb[u][t].astype(F32)
        places = UNITS[u][2]
        return acc[: places * KW * 8].reshape(places, KW, 8, BR)

    send(core_copy(0))

    @pl.loop(1, 8)
    def _(i):
        wspread_land(i)

    fetches[3].wait()
    wcat = [jnp.concatenate([wbuf[slot, k] for k in range(KW)], axis=1) for slot in range(NX)]
    for s in range(NS):
        back = None
        for slot in range(NX):
            part = lax.dot_general(
                gst[slot, s], wcat[slot], (((1,), (1,)), ((), ())), preferred_element_type=F32
            )
            back = part if back is None else back + part
        g1[s, PAD : PAD + LEN, :] = (
            gbuf[0, s, PAD : PAD + LEN, :].astype(F32) + slope[s * LEN : (s + 1) * LEN, :] * back
        ).astype(BF16)
    to_major(0)
    stack(g1, NX, 4)

    def first_piece(place):
        put_piece(0, place, hbuf.at[PLACES[place]], NX)

    xland(hpiece, hs_sem, hr_sem, 0)
    send(xcopy(hpiece, hs_sem, hr_sem, 5))
    xland(hpiece, hs_sem, hr_sem, 2)
    send(xcopy(hpiece, hs_sem, hr_sem, 4))
    first_piece(0)

    def vcopy(i, land):
        q = (p + i) % NX
        at = i if land else NX - i
        return rcopy(rprev.at[at] if land else rprev.at[0], rprev.at[at], vs_sem.at[i], vr_sem.at[at], (dp, q))

    fetches[5].wait()
    for i in range(1, NX):
        send(vcopy(i, False))
    xland(hpiece, hs_sem, hr_sem, 1)
    first_piece(1)
    xland(hpiece, hs_sem, hr_sem, 3)
    first_piece(2)
    send(core_copy(1))
    to_major(1)
    xland(hpiece, hs_sem, hr_sem, 4)
    xland(hpiece, hs_sem, hr_sem, 5)
    first_piece(3)
    send(core_copy(2))
    to_major(2)
    to_minor(0)
    to_minor(1)
    to_minor(2)

    acc = minor_sum(0)
    for place in range(NX):
        p3[PLACES[place]] = acc[place]

    def piece_copy(i, land):
        q = (p + i) % NX
        return rcopy(
            r3.at[q] if land else p3.at[i], r3.at[q if land else p],
            s3_sem.at[i], r3_sem.at[q if land else p], (dp, q),
        )

    for i in range(1, NX):
        send(piece_copy(i, False))
    for u in (1, 2):
        acc = minor_sum(u)
        for k in range(UNITS[u][2]):
            q = (p + PLACES[UNITS[u][1] + k]) % NX
            rows_ref[pl.ds(q * KW, KW)] = acc[k]
    rows_ref[pl.ds((NX + p) * KW, KW)] = p3[0]
    for i in range(1, NX):
        piece_copy(i, True).wait_recv()
        q = (p + i) % NX
        rows_ref[pl.ds((NX + q) * KW, KW)] = r3[q]

    def line(i):
        return peer_at(i // 2, b, c) - c + i % 2

    for i in range(16):
        d4[i] = rows_ref[bos_ref[line(i)]]

    def group_copy(j):
        i = (a * 2 + c + j) % 16
        me = c * 8 + a
        return rcopy(d4.at[i], f4.at[me], fs_sem.at[i], fr_sem.at[me], (line(i), p))

    @pl.loop(1, 16)
    def _(j):
        group_copy(j).start()

    loops.append((16, group_copy))
    f4[c * 8 + a] = d4[a * 2 + c]

    @pl.loop(1, 16)
    def _(j):
        i = (c * 8 + a + j) % 16
        rcopy(f4.at[i], f4.at[i], fs_sem.at[i], fr_sem.at[i], (sib, p)).wait_recv()

    tiles[0] = f4[...].reshape(BR, BR).astype(BF16)

    def tile_copy(i, land):
        q = (p + i) % NX
        at = i if land else NX - i
        return rcopy(tiles.at[at] if land else tiles.at[0], tiles.at[at], ts_sem.at[i], tr_sem.at[at], (dp, q))

    for i in range(1, NX):
        send(tile_copy(i, False))
    for i in range(1, NX):
        vcopy(i, True).wait_recv()
    fetches[4].wait()
    for i in range(1, NX):
        tile_copy(i, True).wait_recv()

    tile = [tiles[i] for i in range(NX)]
    left_sum = None
    stats = []
    for i in range(NX):
        part = lax.dot_general(tile[i], tile[i], (((1,), (1,)), ((), ())), preferred_element_type=F32)
        left_sum = part if left_sum is None else left_sum + part
        gram = lax.dot_general(tile[i], tile[i], (((0,), (0,)), ((), ())), preferred_element_type=F32)
        stats.append(DECAY * rprev[i] + (1.0 - DECAY) * gram)
    stats.append(DECAY * lprev_ref[...] + (1.0 - DECAY) * left_sum)
    roots = [split(r) for r in inverse_fourth_roots(stats)]
    left_root = roots[NX]
    zero = jnp.zeros((BR, BR), BF16)
    raw = []
    for i in range(NX):
        mixed = split(mm(left_root, (tile[i], zero)) + mm((tile[i], zero), roots[i]))
        raw.append(mm(left_root, mixed) + mm(mixed, roots[i]))
    squares = raw[0] * raw[0]
    for i in range(1, NX):
        squares = squares + raw[i] * raw[i]
    total = jnp.sum(squares, axis=(0, 1), keepdims=True)
    inv = 1.0 / jnp.sqrt(total / (NX * BR * BR) + 1e-6)
    out_ref[...] = jnp.where(cnt_ref[0] > 0, raw[0] * inv, 0.0)

    drain()


def local(
    block_input, block_middle, out_grad, lengths, conv_weight, block_of_slot, slot_count, left_prev, right_prev
):
    vmem = pl.BlockSpec(memory_space=pltpu.VMEM)
    smem = pl.BlockSpec(memory_space=pltpu.SMEM)
    hbm = pl.BlockSpec(memory_space=pltpu.HBM)
    dma = pltpu.SemaphoreType.DMA
    out = pl.pallas_call(
        kernel,
        out_shape=jax.ShapeDtypeStruct((BR, BR), F32),
        in_specs=[hbm, hbm, hbm, smem, hbm, smem, smem, hbm, hbm],
        out_specs=vmem,
        scratch_shapes=[
            pltpu.VMEM((NS * LEN, BR), BF16),
            pltpu.VMEM((NS * LEN, BR), BF16),
            pltpu.VMEM((NS * LEN, BR), BF16),
            pltpu.VMEM((BR, BR), F32),
            pltpu.VMEM((NX, BR, BR), F32),
            pltpu.VMEM((NX, NS, LEN + 2 * PAD, BR), BF16),
            pltpu.VMEM((NX, NS, BR, LEN), BF16),
            pltpu.VMEM((NS, BR, LEN), BF16),
            pltpu.VMEM((NS * LEN, BR), F32),
            pltpu.VMEM((NX, KW, BR, BR), BF16),
            pltpu.VMEM((NX + 1, NS, LEN, KW * BR), BF16),
            pltpu.VMEM((NS, LEN + 2 * PAD, BR), BF16),
            pltpu.VMEM((2, NX, KW * BR, BR), F32),
            *[pltpu.VMEM((n * KW, 64, BR), F32) for _, _, n in UNITS],
            *[pltpu.VMEM((8, padded_rows(n), BR), BF16) for _, _, n in UNITS],
            *[pltpu.VMEM((8, padded_rows(n), BR), BF16) for _, _, n in UNITS],
            *[pltpu.VMEM((padded_rows(n), BR), BF16) for _, _, n in UNITS],
            *[pltpu.VMEM((8, padded_rows(n), BR), BF16) for _, _, n in UNITS],
            pltpu.VMEM((NX, KW, 8, BR), F32),
            pltpu.VMEM((NX, KW, 8, BR), F32),
            pltpu.VMEM((2 * NX * KW, 8, BR), F32),
            pltpu.VMEM((16, 8, BR), F32),
            pltpu.VMEM((16, 8, BR), F32),
            pltpu.VMEM((NX, BR, BR), BF16),
            dma((6,)), dma((6,)), dma((6,)), dma((6,)), dma((NX,)), dma((NX,)), dma((8,)), dma((8,)), dma((6,)),
            dma((3, 8)), dma((3, 8)), dma((3, 8)), dma((3, 8)), dma((NX,)), dma((NX,)),
            dma((16,)), dma((16,)), dma((NX,)), dma((NX,)), dma((NX,)), dma((NX,)), dma((6,)),
        ],
        compiler_params=pltpu.CompilerParams(
            collective_id=0, has_side_effects=True, vmem_limit_bytes=60 * 1024 * 1024
        ),
    )(
        block_input, block_middle, out_grad, lengths, conv_weight.transpose(1, 0, 2), block_of_slot,
        slot_count, left_prev.reshape(BR, BR), right_prev.reshape(BR, BR),
    )
    return out.reshape(1, BR * BR)


def solution(mesh):
    return jax.shard_map(
        local,
        mesh=mesh,
        in_specs=(
            P("dp", "owner"), P("dp", "owner"), P("dp", "owner"), P("dp"), P(None, None, "owner"), P(),
            P("dp"), P("dp", None), P("dp", "owner"),
        ),
        out_specs=P("dp", "owner"),
        check_vma=False,
    )
```

```python
import jax
import jax.numpy as jnp
from jax import lax
from jax.experimental import pallas as pl
from jax.experimental.pallas import tpu as pltpu
from jax.sharding import PartitionSpec as P

MESH = pl.DeviceIdType.MESH
F32, BF16 = jnp.float32, jnp.bfloat16
KW = 5
BR = 128
LEN = 512
PAD = 16
NS = 2
NX, NY, NZ = 4, 8, 8
ITERS = 8
DECAY = 0.9


def split(a):
    high = a.astype(BF16)
    return high, (a - high.astype(F32)).astype(BF16)


def mm(a, b):
    (ah, al), (bh, bl) = a, b
    left = jnp.concatenate([ah, al], axis=1)
    right = jnp.concatenate(
        [jnp.concatenate([bh, bl], axis=1), jnp.concatenate([bh, jnp.zeros_like(bl)], axis=1)], axis=0
    )
    both = jnp.dot(left, right, preferred_element_type=F32)
    return both[:, :BR] + both[:, BR:]


def inverse_fourth_roots(stats):
    rows = lax.broadcasted_iota(jnp.int32, (BR, BR), 0)
    cols = lax.broadcasted_iota(jnp.int32, (BR, BR), 1)
    eye = (rows == cols).astype(F32)
    norms = [jnp.sqrt(jnp.sum(s * s, axis=(0, 1), keepdims=True)) for s in stats]
    cur = [s / n for s, n in zip(stats, norms)]
    root = None
    for it in range(ITERS):
        fac = [1.25 * eye - 0.25 * m for m in cur]
        parts = [split(f) for f in fac]
        if it < ITERS - 1:
            square = [split(mm(f, f)) for f in parts]
            fourth = [split(mm(s, s)) for s in square]
            cur = [mm(f, split(m)) for f, m in zip(fourth, cur)]
        root = fac if it == 0 else [mm(split(r), f) for r, f in zip(root, parts)]
    scale = [1.0 / jnp.sqrt(jnp.sqrt(n)) for n in norms]
    return [r * s for r, s in zip(root, scale)]


def peer_at(major, minor, core):
    z = major + core * (minor - major)
    y = minor + core * (major - minor)
    return (z * NY + y) * 2 + core


PLACES = (0, 3, 1, 2)
UNITS = ((1, 0, 3), (1, 3, 1), (0, 0, 3), (0, 3, 1))
FAR = (4, 3, 5, 2, 6, 1, 7)


def padded_rows(places):
    return -(-places * KW * 8 // 16) * 16


def kernel(
    x1_hbm, x2_hbm, g_hbm, len_hbm, w_ref, bos_hbm, cnt_hbm, lprev_hbm, rprev_hbm, out_ref,
    len_ref, bos_ref, cnt_ref, x1_ref, x2_ref, g_ref, lprev_ref, rprev,
    gbuf, hbuf, h2t, slope, wbuf, gst, g1, kbuf,
    c0, c1, c2, c3, pa0, pa1, pa2, pa3, ra0, ra1, ra2, ra3, pb0, pb1, pb2, pb3, rb0, rb1, rb2, rb3, p3, r3, rows_ref, d4, f4, tiles,
    gs_sem, gr_sem, hs_sem, hr_sem, ws_sem, wr_sem, as_sem, ar_sem, c0_sem, s1_sem, r1_sem, s2_sem, r2_sem,
    s3_sem, r3_sem, fs_sem, fr_sem, vs_sem, vr_sem, ts_sem, tr_sem, in_sem,
):
    dp, p = lax.axis_index("dp"), lax.axis_index("owner")
    c = dp % 2
    y = (dp // 2) % NY
    z = dp // (2 * NY)
    a = z + c * (y - z)
    b = y + c * (z - y)
    right, left = (p + 1) % NX, (p + 3) % NX
    core_in, pa, ra = (c0, c1, c2, c3), (pa0, pa1, pa2, pa3), (ra0, ra1, ra2, ra3)
    pb, rb = (pb0, pb1, pb2, pb3), (rb0, rb1, rb2, rb3)

    barrier = pltpu.get_barrier_semaphore()

    def greet(dev):
        pl.semaphore_signal(barrier, inc=1, device_id=dev, device_id_type=MESH)

    for step in FAR:
        for core in range(2):
            greet(((z * NY + (y + step) % NY) * 2 + core, p))
    for step in (2, 1, 3):
        greet((dp, (p + step) % NX))
    for step in FAR:
        for core in range(2):
            greet(((((z + step) % NZ) * NY + y) * 2 + core, p))
    greet((dp + 1 - 2 * c, p))

    def rcopy(src, dst, ss, rs, dev):
        return pltpu.make_async_remote_copy(
            src_ref=src, dst_ref=dst, send_sem=ss, recv_sem=rs, device_id=dev, device_id_type=MESH
        )

    def fetch(i, src, dst):
        return pltpu.make_async_copy(src, dst, in_sem.at[i])

    own = pl.ds(pl.multiple_of(p * BR, BR), BR)
    fetches = [
        fetch(0, g_hbm, g_ref), fetch(1, x1_hbm, x1_ref), fetch(2, x2_hbm, x2_ref),
        fetch(3, w_ref.at[:, own, :], wbuf.at[0]), fetch(4, lprev_hbm, lprev_ref), fetch(5, rprev_hbm, rprev.at[0]),
        fetch(6, len_hbm, len_ref), fetch(7, bos_hbm, bos_ref), fetch(8, cnt_hbm, cnt_ref),
    ]
    for i in (6, 0, 1, 2, 3, 4, 5, 7, 8):
        fetches[i].start()

    sent = []

    def send(copy):
        copy.start()
        sent.append(copy)

    def drain():
        for copy in sent:
            copy.wait_send()

    zpad = jnp.zeros((PAD, BR), BF16)
    for slot in range(NX):
        for s in range(NS):
            gbuf[slot, s, 0:PAD, :] = zpad
            gbuf[slot, s, PAD + LEN : PAD + LEN + PAD, :] = zpad
    for s in range(NS):
        g1[s, 0:PAD, :] = zpad
        g1[s, PAD + LEN : PAD + LEN + PAD, :] = zpad
    tok = lax.broadcasted_iota(jnp.int32, (LEN, BR), 0)
    fetches[6].wait()
    fetches[0].wait()
    for s in range(NS):
        v = g_ref[s * LEN : (s + 1) * LEN, :].astype(F32)
        gbuf[0, s, PAD : PAD + LEN, :] = jnp.where(tok < len_ref[s], v, 0.0).astype(BF16)

    pl.semaphore_wait(barrier, 3 + 15 + 14)

    def gpiece(slot, s):
        return gbuf.at[slot, s, pl.ds(PAD, LEN), :]

    def hpiece(slot, s):
        return hbuf.at[slot, s]

    plan = [
        (0, 3, 1, right), (0, 3, 0, right), (0, 1, 0, left), (0, 1, 1, left),
        (1, 2, 0, left), (3, 2, 1, right),
    ]

    def xcopy(piece, ss, rs, i):
        src, dst, s, dev = plan[i]
        return rcopy(piece(src, s), piece(dst, s), ss.at[i], rs.at[i], (dp, dev))

    def xland(piece, ss, rs, i):
        src, dst, s, dev = plan[i]
        rcopy(piece(dst, s), piece(dst, s), ss.at[i], rs.at[i], (dp, dev)).wait_recv()

    def wcopy(i):
        q = (p + i) % NX
        src = w_ref.at[:, pl.ds(pl.multiple_of(q * BR + a * 16, 16), 16), :]
        dst = wbuf.at[NX - i, :, pl.ds(pl.multiple_of(a * 16, 16), 16), :]
        return rcopy(src, dst, ws_sem.at[NX - i], wr_sem.at[NX - i], (dp, q))

    def wpart(t):
        return wbuf.at[pl.ds(1, NX - 1), :, pl.ds(pl.multiple_of(t * 16, 16), 16), :]

    def wspread(i):
        t = (a + i) % 8
        return rcopy(wpart(a), wpart(a), as_sem.at[t], ar_sem.at[a], (peer_at(t, b, c), p))

    def wspread_land(i):
        t = (a + i) % 8
        rcopy(wpart(t), wpart(t), as_sem.at[t], ar_sem.at[t], (peer_at(t, b, c), p)).wait_recv()

    for i in (0, 2, 1, 3):
        send(xcopy(gpiece, gs_sem, gr_sem, i))
    for i in (2, 1, 3):
        send(wcopy(i))

    fetches[1].wait()

    @pl.loop(0, NS * LEN // BR)
    def _(i):
        s = i // (LEN // BR)
        t0 = pl.multiple_of((i % (LEN // BR)) * BR, BR)
        r0 = pl.multiple_of(i * BR, BR)
        valid = (lax.broadcasted_iota(jnp.int32, (BR, BR), 0) + t0 < len_ref[s]).astype(F32)
        x = x1_ref[pl.ds(r0, BR), :].astype(F32)
        h = x * (0.5 * (1.0 + lax.erf(x * 0.7071067811865476))) * valid
        hbuf[0, s, :, pl.ds(t0, BR)] = h.T.astype(BF16)

    fetches[2].wait()

    @pl.loop(0, NS * LEN // BR)
    def _(i):
        s = i // (LEN // BR)
        t0 = pl.multiple_of((i % (LEN // BR)) * BR, BR)
        r0 = pl.multiple_of(i * BR, BR)
        valid = (lax.broadcasted_iota(jnp.int32, (BR, BR), 0) + t0 < len_ref[s]).astype(F32)
        x = x2_ref[pl.ds(r0, BR), :].astype(F32)
        phi = 0.5 * (1.0 + lax.erf(x * 0.7071067811865476))
        h2t[s, :, pl.ds(t0, BR)] = (x * phi * valid).T.astype(BF16)
        slope[pl.ds(r0, BR), :] = (phi + x * jnp.exp(-0.5 * x * x) * 0.3989422804014327) * valid

    def stack(src, slot, dilation):
        for s in range(NS):
            for k in range(KW):
                r0 = PAD - (k - KW // 2) * dilation
                gst[slot, s, :, k * BR : (k + 1) * BR] = src[s, r0 : r0 + LEN, :]

    def put_piece(kk, place, acts, slot):
        prod = jnp.dot(acts[0], gst[slot, 0], preferred_element_type=F32)
        prod += jnp.dot(acts[1], gst[slot, 1], preferred_element_type=F32)
        for k in range(KW):
            kbuf[kk, place, pl.ds(k, BR, stride=KW), :] = prod[:, k * BR : (k + 1) * BR]

    def second_piece(place):
        stack(gbuf.at[PLACES[place]], PLACES[place], 8)
        put_piece(1, place, h2t, PLACES[place])

    sib = dp + 1 - 2 * c

    def ktile(u):
        kk, first, places = UNITS[u]
        return kbuf.at[kk].reshape(NX * KW, BR, BR).at[pl.ds(first * KW, places * KW)]

    def core_copy(u):
        other = pl.ds(pl.multiple_of((1 - c) * 64, 64), 64)
        return rcopy(
            ktile(u).at[:, other, :], core_in[u], c0_sem.at[2 * u], c0_sem.at[2 * u + 1], (sib, p)
        )

    def major_copy(u, t, land):
        return rcopy(
            ra[u].at[t] if land else pa[u].at[t], ra[u].at[t if land else a],
            s1_sem.at[u, t], r1_sem.at[u, t if land else a], (peer_at(t, b, c), p),
        )

    def minor_copy(u, t, land):
        return rcopy(
            rb[u].at[t] if land else pb[u], rb[u].at[t if land else b],
            s2_sem.at[u, t], r2_sem.at[u, t if land else b], (peer_at(a, t, c), p),
        )

    def to_major(u):
        core_copy(u).wait_recv()
        rows = UNITS[u][2] * KW * 8
        mine = pl.multiple_of(c * 64, 64)

        @pl.loop(0, 8)
        def _(t):
            t8 = pl.multiple_of(t * 8, 8)
            both = ktile(u)[:, pl.ds(mine + t8, 8), :] + core_in[u][:, pl.ds(t8, 8), :]
            both = both.reshape(rows, BR)
            if padded_rows(UNITS[u][2]) > rows:
                both = jnp.concatenate([both, jnp.zeros((8, BR), F32)], axis=0)
            pa[u][t] = both.astype(BF16)

        for step in FAR:
            send(major_copy(u, (a + step) % 8, False))

    def to_minor(u):
        acc = pa[u][a].astype(F32)
        for i in range(1, 8):
            t = (a + i) % 8
            major_copy(u, t, True).wait_recv()
            acc = acc + ra[u][t].astype(F32)
        pb[u][...] = acc.astype(BF16)

        for step in FAR:
            send(minor_copy(u, (b + step) % 8, False))

    def minor_sum(u):
        acc = pb[u][...].astype(F32)
        for i in range(1, 8):
            t = (b + i) % 8
            minor_copy(u, t, True).wait_recv()
            acc = acc + rb[u][t].astype(F32)
        places = UNITS[u][2]
        return acc[: places * KW * 8].reshape(places, KW, 8, BR)

    def vcopy(i, land):
        q = (p + i) % NX
        at = i if land else NX - i
        return rcopy(rprev.at[at] if land else rprev.at[0], rprev.at[at], vs_sem.at[i], vr_sem.at[at], (dp, q))

    def piece_copy(i, land):
        q = (p + i) % NX
        return rcopy(
            r3.at[q] if land else p3.at[i], r3.at[q if land else p],
            s3_sem.at[i], r3_sem.at[q if land else p], (dp, q),
        )


    def first_piece(place):
        put_piece(0, place, hbuf.at[PLACES[place]], NX)

    def cotangent(s):
        back = None
        for slot in range(NX):
            wcat = jnp.concatenate([wbuf[slot, k] for k in range(KW)], axis=1)
            part = lax.dot_general(gst[slot, s], wcat, (((1,), (1,)), ((), ())), preferred_element_type=F32)
            back = part if back is None else back + part
        g1[s, PAD : PAD + LEN, :] = (
            gbuf[0, s, PAD : PAD + LEN, :].astype(F32) + slope[s * LEN : (s + 1) * LEN, :] * back
        ).astype(BF16)

    second_piece(0)
    for i in range(1, NX):
        wcopy(i).wait_recv()
    for step in FAR:
        send(wspread(step))
    xland(gpiece, gs_sem, gr_sem, 0)
    send(xcopy(gpiece, gs_sem, gr_sem, 5))
    xland(gpiece, gs_sem, gr_sem, 2)
    send(xcopy(gpiece, gs_sem, gr_sem, 4))
    xland(gpiece, gs_sem, gr_sem, 1)
    xland(gpiece, gs_sem, gr_sem, 3)
    for i in (0, 2, 1, 3):
        send(xcopy(hpiece, hs_sem, hr_sem, i))
    second_piece(1)
    second_piece(2)
    send(core_copy(0))
    xland(gpiece, gs_sem, gr_sem, 4)
    xland(gpiece, gs_sem, gr_sem, 5)
    second_piece(3)
    send(core_copy(1))
    to_major(0)

    @pl.loop(1, 8)
    def _(i):
        wspread_land(i)

    fetches[3].wait()
    cotangent(0)
    to_major(1)
    cotangent(1)
    stack(g1, NX, 4)
    first_piece(0)
    xland(hpiece, hs_sem, hr_sem, 0)
    send(xcopy(hpiece, hs_sem, hr_sem, 5))
    xland(hpiece, hs_sem, hr_sem, 2)
    send(xcopy(hpiece, hs_sem, hr_sem, 4))
    xland(hpiece, hs_sem, hr_sem, 1)
    first_piece(1)
    xland(hpiece, hs_sem, hr_sem, 3)
    first_piece(2)
    send(core_copy(2))
    to_minor(0)
    to_major(2)
    xland(hpiece, hs_sem, hr_sem, 4)
    xland(hpiece, hs_sem, hr_sem, 5)
    first_piece(3)
    send(core_copy(3))
    fetches[5].wait()
    for i in (2, 1, 3):
        send(vcopy(i, False))
    to_minor(1)
    to_major(3)
    to_minor(2)

    for u in (0, 1):
        acc = minor_sum(u)
        for k in range(UNITS[u][2]):
            p3[PLACES[UNITS[u][1] + k]] = acc[k]
    for i in (2, 1, 3):
        send(piece_copy(i, False))
    to_minor(3)
    rows_ref[pl.ds((NX + p) * KW, KW)] = p3[0]
    for i in range(1, NX):
        piece_copy(i, True).wait_recv()
        q = (p + i) % NX
        rows_ref[pl.ds((NX + q) * KW, KW)] = r3[q]
    for u in (2, 3):
        acc = minor_sum(u)
        for k in range(UNITS[u][2]):
            q = (p + PLACES[UNITS[u][1] + k]) % NX
            rows_ref[pl.ds(q * KW, KW)] = acc[k]

    def line(i):
        return peer_at(i // 2, b, c) - c + i % 2

    fetches[7].wait()
    for i in range(16):
        d4[i] = rows_ref[bos_ref[line(i)]]

    def group_copy(i):
        me = c * 8 + a
        return rcopy(d4.at[i], f4.at[me], fs_sem.at[i], fr_sem.at[me], (line(i), p))

    for step in FAR:
        for core in range(2):
            send(group_copy((a + step) % 8 * 2 + core))
    send(group_copy(a * 2 + 1 - c))
    f4[c * 8 + a] = d4[a * 2 + c]

    @pl.loop(1, 16)
    def _(j):
        i = (c * 8 + a + j) % 16
        rcopy(f4.at[i], f4.at[i], fs_sem.at[i], fr_sem.at[i], (sib, p)).wait_recv()

    tiles[0] = f4[...].reshape(BR, BR).astype(BF16)

    def tile_copy(i, land):
        q = (p + i) % NX
        at = i if land else NX - i
        return rcopy(tiles.at[at] if land else tiles.at[0], tiles.at[at], ts_sem.at[i], tr_sem.at[at], (dp, q))

    for i in (2, 1, 3):
        send(tile_copy(i, False))
    for i in range(1, NX):
        vcopy(i, True).wait_recv()
    fetches[4].wait()
    fetches[8].wait()
    for i in range(1, NX):
        tile_copy(i, True).wait_recv()

    tile = [tiles[i] for i in range(NX)]
    left_sum = None
    stats = []
    for i in range(NX):
        part = lax.dot_general(tile[i], tile[i], (((1,), (1,)), ((), ())), preferred_element_type=F32)
        left_sum = part if left_sum is None else left_sum + part
        gram = lax.dot_general(tile[i], tile[i], (((0,), (0,)), ((), ())), preferred_element_type=F32)
        stats.append(DECAY * rprev[i] + (1.0 - DECAY) * gram)
    stats.append(DECAY * lprev_ref[...] + (1.0 - DECAY) * left_sum)
    roots = [split(r) for r in inverse_fourth_roots(stats)]
    left_root = roots[NX]
    zero = jnp.zeros((BR, BR), BF16)
    raw = []
    for i in range(NX):
        mixed = split(mm(left_root, (tile[i], zero)) + mm((tile[i], zero), roots[i]))
        raw.append(mm(left_root, mixed) + mm(mixed, roots[i]))
    squares = raw[0] * raw[0]
    for i in range(1, NX):
        squares = squares + raw[i] * raw[i]
    total = jnp.sum(squares, axis=(0, 1), keepdims=True)
    inv = 1.0 / jnp.sqrt(total / (NX * BR * BR) + 1e-6)
    out_ref[...] = jnp.where(cnt_ref[0] > 0, raw[0] * inv, 0.0)

    drain()


def local(
    block_input, block_middle, out_grad, lengths, conv_weight, block_of_slot, slot_count, left_prev, right_prev
):
    vmem = pl.BlockSpec(memory_space=pltpu.VMEM)
    hbm = pl.BlockSpec(memory_space=pltpu.HBM)
    dma = pltpu.SemaphoreType.DMA
    out = pl.pallas_call(
        kernel,
        out_shape=jax.ShapeDtypeStruct((BR, BR), F32),
        in_specs=[hbm] * 9,
        out_specs=vmem,
        scratch_shapes=[
            pltpu.SMEM((NS,), jnp.int32),
            pltpu.SMEM((BR,), jnp.int32),
            pltpu.SMEM((1,), jnp.int32),
            pltpu.VMEM((NS * LEN, BR), BF16),
            pltpu.VMEM((NS * LEN, BR), BF16),
            pltpu.VMEM((NS * LEN, BR), BF16),
            pltpu.VMEM((BR, BR), F32),
            pltpu.VMEM((NX, BR, BR), F32),
            pltpu.VMEM((NX, NS, LEN + 2 * PAD, BR), BF16),
            pltpu.VMEM((NX, NS, BR, LEN), BF16),
            pltpu.VMEM((NS, BR, LEN), BF16),
            pltpu.VMEM((NS * LEN, BR), F32),
            pltpu.VMEM((NX, KW, BR, BR), BF16),
            pltpu.VMEM((NX + 1, NS, LEN, KW * BR), BF16),
            pltpu.VMEM((NS, LEN + 2 * PAD, BR), BF16),
            pltpu.VMEM((2, NX, KW * BR, BR), F32),
            *[pltpu.VMEM((n * KW, 64, BR), F32) for _, _, n in UNITS],
            *[pltpu.VMEM((8, padded_rows(n), BR), BF16) for _, _, n in UNITS],
            *[pltpu.VMEM((8, padded_rows(n), BR), BF16) for _, _, n in UNITS],
            *[pltpu.VMEM((padded_rows(n), BR), BF16) for _, _, n in UNITS],
            *[pltpu.VMEM((8, padded_rows(n), BR), BF16) for _, _, n in UNITS],
            pltpu.VMEM((NX, KW, 8, BR), F32),
            pltpu.VMEM((NX, KW, 8, BR), F32),
            pltpu.VMEM((2 * NX * KW, 8, BR), F32),
            pltpu.VMEM((16, 8, BR), F32),
            pltpu.VMEM((16, 8, BR), F32),
            pltpu.VMEM((NX, BR, BR), BF16),
            dma((6,)), dma((6,)), dma((6,)), dma((6,)), dma((NX,)), dma((NX,)), dma((8,)), dma((8,)), dma((8,)),
            dma((4, 8)), dma((4, 8)), dma((4, 8)), dma((4, 8)), dma((NX,)), dma((NX,)),
            dma((16,)), dma((16,)), dma((NX,)), dma((NX,)), dma((NX,)), dma((NX,)), dma((9,)),
        ],
        compiler_params=pltpu.CompilerParams(
            collective_id=0, has_side_effects=True, vmem_limit_bytes=60 * 1024 * 1024
        ),
    )(
        block_input, block_middle, out_grad, lengths, conv_weight.transpose(1, 0, 2), block_of_slot,
        slot_count, left_prev.reshape(BR, BR), right_prev.reshape(BR, BR),
    )
    return out.reshape(1, BR * BR)


def solution(mesh):
    return jax.shard_map(
        local,
        mesh=mesh,
        in_specs=(
            P("dp", "owner"), P("dp", "owner"), P("dp", "owner"), P("dp"), P(None, None, "owner"), P(),
            P("dp"), P("dp", None), P("dp", "owner"),
        ),
        out_specs=P("dp", "owner"),
        check_vma=False,
    )
```

```python
import jax
import jax.numpy as jnp
from jax import lax
from jax.experimental import pallas as pl
from jax.experimental.pallas import tpu as pltpu
from jax.sharding import PartitionSpec as P

MESH = pl.DeviceIdType.MESH
F32, BF16 = jnp.float32, jnp.bfloat16
KW = 5
BR = 128
LEN = 512
PAD = 16
NS = 2
NX, NY, NZ = 4, 8, 8
ITERS = 8
DECAY = 0.9


def split(a):
    high = a.astype(BF16)
    return high, (a - high.astype(F32)).astype(BF16)


def mm(a, b):
    (ah, al), (bh, bl) = a, b
    left = jnp.concatenate([ah, al], axis=1)
    right = jnp.concatenate(
        [jnp.concatenate([bh, bl], axis=1), jnp.concatenate([bh, jnp.zeros_like(bl)], axis=1)], axis=0
    )
    both = jnp.dot(left, right, preferred_element_type=F32)
    return both[:, :BR] + both[:, BR:]


def bdot(a, b):
    return jnp.dot(a, b, preferred_element_type=F32)


def inverse_fourth_roots(stats):
    rows = lax.broadcasted_iota(jnp.int32, (BR, BR), 0)
    cols = lax.broadcasted_iota(jnp.int32, (BR, BR), 1)
    eye = (rows == cols).astype(F32)
    norms = [jnp.sqrt(jnp.sum(s * s, axis=(0, 1), keepdims=True)) for s in stats]
    cur = [s / n for s, n in zip(stats, norms)]
    root = None
    for it in range(ITERS):
        fac = [1.25 * eye - 0.25 * m for m in cur]
        parts = [split(f) for f in fac]
        if it < ITERS - 1:
            square = [split(mm(f, f)) for f in parts]
            half = [split(mm(s, split(m))) for s, m in zip(square, cur)]
            cur = [mm(h, s) for h, s in zip(half, square)]
        root = fac if it == 0 else [mm(split(r), f) for r, f in zip(root, parts)]
    scale = [1.0 / jnp.sqrt(jnp.sqrt(n)) for n in norms]
    return [r * s for r, s in zip(root, scale)]


def peer_at(major, minor, core):
    z = major + core * (minor - major)
    y = minor + core * (major - minor)
    return (z * NY + y) * 2 + core


PLACES = (0, 3, 1, 2)
UNITS = ((1, 0, 3), (1, 3, 1), (0, 0, 3), (0, 3, 1))
FAR = (4, 3, 5, 2, 6, 1, 7)


def padded_rows(places):
    return -(-places * KW * 8 // 16) * 16


def kernel(
    x1_hbm, x2_hbm, g_hbm, len_hbm, w_ref, bos_hbm, cnt_hbm, lprev_hbm, rprev_hbm, out_ref,
    len_ref, bos_ref, cnt_ref, x1_ref, x2_ref, g_ref, lprev_ref, rprev,
    gbuf, hbuf, h2t, slope, wbuf, gst, g1, kbuf,
    c0, c1, c2, c3, pa0, pa1, pa2, pa3, ra0, ra1, ra2, ra3, pb0, pb1, pb2, pb3, rb0, rb1, rb2, rb3, p3, r3, rows_ref, d4, f4, tiles,
    gs_sem, gr_sem, hs_sem, hr_sem, ws_sem, wr_sem, as_sem, ar_sem, c0_sem, s1_sem, r1_sem, s2_sem, r2_sem,
    s3_sem, r3_sem, fs_sem, fr_sem, vs_sem, vr_sem, ts_sem, tr_sem, in_sem,
):
    dp, p = lax.axis_index("dp"), lax.axis_index("owner")
    c = dp % 2
    y = (dp // 2) % NY
    z = dp // (2 * NY)
    a = z + c * (y - z)
    b = y + c * (z - y)
    right, left = (p + 1) % NX, (p + 3) % NX
    core_in, pa, ra = (c0, c1, c2, c3), (pa0, pa1, pa2, pa3), (ra0, ra1, ra2, ra3)
    pb, rb = (pb0, pb1, pb2, pb3), (rb0, rb1, rb2, rb3)

    barrier = pltpu.get_barrier_semaphore()

    def greet(dev):
        pl.semaphore_signal(barrier, inc=1, device_id=dev, device_id_type=MESH)

    for step in FAR:
        for core in range(2):
            greet(((z * NY + (y + step) % NY) * 2 + core, p))
    for step in (2, 1, 3):
        greet((dp, (p + step) % NX))
    for step in FAR:
        for core in range(2):
            greet(((((z + step) % NZ) * NY + y) * 2 + core, p))
    greet((dp + 1 - 2 * c, p))

    def rcopy(src, dst, ss, rs, dev):
        return pltpu.make_async_remote_copy(
            src_ref=src, dst_ref=dst, send_sem=ss, recv_sem=rs, device_id=dev, device_id_type=MESH
        )

    def fetch(i, src, dst):
        return pltpu.make_async_copy(src, dst, in_sem.at[i])

    own = pl.ds(pl.multiple_of(p * BR, BR), BR)
    fetches = [
        fetch(0, g_hbm, g_ref), fetch(1, x1_hbm, x1_ref), fetch(2, x2_hbm, x2_ref),
        fetch(3, w_ref.at[:, own, :], wbuf.at[0]), fetch(4, lprev_hbm, lprev_ref), fetch(5, rprev_hbm, rprev.at[0]),
        fetch(6, len_hbm, len_ref), fetch(7, bos_hbm, bos_ref), fetch(8, cnt_hbm, cnt_ref),
    ]
    for i in (6, 0, 1, 2, 3, 4, 5, 7, 8):
        fetches[i].start()

    sent = []

    def send(copy):
        copy.start()
        sent.append(copy)

    def drain():
        for copy in sent:
            copy.wait_send()

    zpad = jnp.zeros((PAD, BR), BF16)
    for slot in range(NX):
        for s in range(NS):
            gbuf[slot, s, 0:PAD, :] = zpad
            gbuf[slot, s, PAD + LEN : PAD + LEN + PAD, :] = zpad
    for s in range(NS):
        g1[s, 0:PAD, :] = zpad
        g1[s, PAD + LEN : PAD + LEN + PAD, :] = zpad
    tok = lax.broadcasted_iota(jnp.int32, (LEN, BR), 0)
    fetches[6].wait()
    fetches[0].wait()
    for s in range(NS):
        v = g_ref[s * LEN : (s + 1) * LEN, :].astype(F32)
        gbuf[0, s, PAD : PAD + LEN, :] = jnp.where(tok < len_ref[s], v, 0.0).astype(BF16)

    pl.semaphore_wait(barrier, 3 + 15 + 14)

    def gpiece(slot, s):
        return gbuf.at[slot, s, pl.ds(PAD, LEN), :]

    def hpiece(slot, s):
        return hbuf.at[slot, s]

    plan = [
        (0, 3, 1, right), (0, 3, 0, right), (0, 1, 0, left), (0, 1, 1, left),
        (1, 2, 0, left), (3, 2, 1, right),
    ]

    def xcopy(piece, ss, rs, i):
        src, dst, s, dev = plan[i]
        return rcopy(piece(src, s), piece(dst, s), ss.at[i], rs.at[i], (dp, dev))

    def xland(piece, ss, rs, i):
        src, dst, s, dev = plan[i]
        rcopy(piece(dst, s), piece(dst, s), ss.at[i], rs.at[i], (dp, dev)).wait_recv()

    def wcopy(i):
        q = (p + i) % NX
        src = w_ref.at[:, pl.ds(pl.multiple_of(q * BR + a * 16, 16), 16), :]
        dst = wbuf.at[NX - i, :, pl.ds(pl.multiple_of(a * 16, 16), 16), :]
        return rcopy(src, dst, ws_sem.at[NX - i], wr_sem.at[NX - i], (dp, q))

    def wpart(t):
        return wbuf.at[pl.ds(1, NX - 1), :, pl.ds(pl.multiple_of(t * 16, 16), 16), :]

    def wspread(i):
        t = (a + i) % 8
        return rcopy(wpart(a), wpart(a), as_sem.at[t], ar_sem.at[a], (peer_at(t, b, c), p))

    def wspread_land(i):
        t = (a + i) % 8
        rcopy(wpart(t), wpart(t), as_sem.at[t], ar_sem.at[t], (peer_at(t, b, c), p)).wait_recv()

    for i in (2, 1, 3):
        send(wcopy(i))
    for i in (0, 2, 1, 3):
        send(xcopy(gpiece, gs_sem, gr_sem, i))

    fetches[1].wait()

    @pl.loop(0, NS * LEN // BR)
    def _(i):
        s = i // (LEN // BR)
        t0 = pl.multiple_of((i % (LEN // BR)) * BR, BR)
        r0 = pl.multiple_of(i * BR, BR)
        valid = (lax.broadcasted_iota(jnp.int32, (BR, BR), 0) + t0 < len_ref[s]).astype(F32)
        x = x1_ref[pl.ds(r0, BR), :].astype(F32)
        h = x * (0.5 * (1.0 + lax.erf(x * 0.7071067811865476))) * valid
        hbuf[0, s, :, pl.ds(t0, BR)] = h.T.astype(BF16)

    fetches[2].wait()

    @pl.loop(0, NS * LEN // BR)
    def _(i):
        s = i // (LEN // BR)
        t0 = pl.multiple_of((i % (LEN // BR)) * BR, BR)
        r0 = pl.multiple_of(i * BR, BR)
        valid = (lax.broadcasted_iota(jnp.int32, (BR, BR), 0) + t0 < len_ref[s]).astype(F32)
        x = x2_ref[pl.ds(r0, BR), :].astype(F32)
        phi = 0.5 * (1.0 + lax.erf(x * 0.7071067811865476))
        h2t[s, :, pl.ds(t0, BR)] = (x * phi * valid).T.astype(BF16)
        slope[pl.ds(r0, BR), :] = (phi + x * jnp.exp(-0.5 * x * x) * 0.3989422804014327) * valid

    def stack(src, slot, dilation):
        for s in range(NS):
            for k in range(KW):
                r0 = PAD - (k - KW // 2) * dilation
                gst[slot, s, :, k * BR : (k + 1) * BR] = src[s, r0 : r0 + LEN, :]

    def put_piece(kk, place, acts, slot):
        prod = jnp.dot(acts[0], gst[slot, 0], preferred_element_type=F32)
        prod += jnp.dot(acts[1], gst[slot, 1], preferred_element_type=F32)
        for k in range(KW):
            kbuf[kk, place, pl.ds(k, BR, stride=KW), :] = prod[:, k * BR : (k + 1) * BR]

    def second_piece(place):
        stack(gbuf.at[PLACES[place]], PLACES[place], 8)
        put_piece(1, place, h2t, PLACES[place])

    sib = dp + 1 - 2 * c

    def ktile(u):
        kk, first, places = UNITS[u]
        return kbuf.at[kk].reshape(NX * KW, BR, BR).at[pl.ds(first * KW, places * KW)]

    def core_copy(u):
        other = pl.ds(pl.multiple_of((1 - c) * 64, 64), 64)
        return rcopy(
            ktile(u).at[:, other, :], core_in[u], c0_sem.at[2 * u], c0_sem.at[2 * u + 1], (sib, p)
        )

    def major_copy(u, t, land):
        return rcopy(
            ra[u].at[t] if land else pa[u].at[t], ra[u].at[t if land else a],
            s1_sem.at[u, t], r1_sem.at[u, t if land else a], (peer_at(t, b, c), p),
        )

    def minor_copy(u, t, land):
        return rcopy(
            rb[u].at[t] if land else pb[u], rb[u].at[t if land else b],
            s2_sem.at[u, t], r2_sem.at[u, t if land else b], (peer_at(a, t, c), p),
        )

    def to_major(u):
        core_copy(u).wait_recv()
        rows = UNITS[u][2] * KW * 8
        mine = pl.multiple_of(c * 64, 64)

        def fill(t):
            t8 = pl.multiple_of(t * 8, 8)
            both = ktile(u)[:, pl.ds(mine + t8, 8), :] + core_in[u][:, pl.ds(t8, 8), :]
            both = both.reshape(rows, BR)
            if padded_rows(UNITS[u][2]) > rows:
                both = jnp.concatenate([both, jnp.zeros((8, BR), F32)], axis=0)
            pa[u][t] = both.astype(BF16)

        for step in FAR:
            t = (a + step) % 8
            fill(t)
            send(major_copy(u, t, False))
        fill(a)

    def to_minor(u):
        acc = pa[u][a].astype(F32)
        for i in range(1, 8):
            t = (a + i) % 8
            major_copy(u, t, True).wait_recv()
            acc = acc + ra[u][t].astype(F32)
        pb[u][...] = acc.astype(BF16)

        for step in FAR:
            send(minor_copy(u, (b + step) % 8, False))

    def minor_sum(u):
        acc = pb[u][...].astype(F32)
        for i in range(1, 8):
            t = (b + i) % 8
            minor_copy(u, t, True).wait_recv()
            acc = acc + rb[u][t].astype(F32)
        places = UNITS[u][2]
        return acc[: places * KW * 8].reshape(places, KW, 8, BR)

    def vcopy(i, land):
        q = (p + i) % NX
        at = i if land else NX - i
        return rcopy(rprev.at[at] if land else rprev.at[0], rprev.at[at], vs_sem.at[i], vr_sem.at[at], (dp, q))

    def piece_copy(i, land):
        q = (p + i) % NX
        return rcopy(
            r3.at[q] if land else p3.at[i], r3.at[q if land else p],
            s3_sem.at[i], r3_sem.at[q if land else p], (dp, q),
        )


    def first_piece(place):
        put_piece(0, place, hbuf.at[PLACES[place]], NX)

    def cotangent(s):
        back = None
        for slot in range(NX):
            wcat = jnp.concatenate([wbuf[slot, k] for k in range(KW)], axis=1)
            part = lax.dot_general(gst[slot, s], wcat, (((1,), (1,)), ((), ())), preferred_element_type=F32)
            back = part if back is None else back + part
        g1[s, PAD : PAD + LEN, :] = (
            gbuf[0, s, PAD : PAD + LEN, :].astype(F32) + slope[s * LEN : (s + 1) * LEN, :] * back
        ).astype(BF16)

    second_piece(0)
    for i in range(1, NX):
        wcopy(i).wait_recv()
    for step in FAR:
        send(wspread(step))
    xland(gpiece, gs_sem, gr_sem, 0)
    send(xcopy(gpiece, gs_sem, gr_sem, 5))
    xland(gpiece, gs_sem, gr_sem, 2)
    send(xcopy(gpiece, gs_sem, gr_sem, 4))
    xland(gpiece, gs_sem, gr_sem, 1)
    xland(gpiece, gs_sem, gr_sem, 3)
    for i in (0, 2, 1, 3):
        send(xcopy(hpiece, hs_sem, hr_sem, i))
    second_piece(1)
    second_piece(2)
    send(core_copy(0))
    xland(gpiece, gs_sem, gr_sem, 4)
    xland(gpiece, gs_sem, gr_sem, 5)
    second_piece(3)
    send(core_copy(1))
    to_major(0)

    @pl.loop(1, 8)
    def _(i):
        wspread_land(i)

    fetches[3].wait()
    cotangent(0)
    to_major(1)
    cotangent(1)
    stack(g1, NX, 4)
    first_piece(0)
    xland(hpiece, hs_sem, hr_sem, 0)
    send(xcopy(hpiece, hs_sem, hr_sem, 5))
    xland(hpiece, hs_sem, hr_sem, 2)
    send(xcopy(hpiece, hs_sem, hr_sem, 4))
    xland(hpiece, hs_sem, hr_sem, 1)
    first_piece(1)
    xland(hpiece, hs_sem, hr_sem, 3)
    first_piece(2)
    send(core_copy(2))
    to_minor(0)
    to_major(2)
    xland(hpiece, hs_sem, hr_sem, 4)
    xland(hpiece, hs_sem, hr_sem, 5)
    first_piece(3)
    send(core_copy(3))
    fetches[5].wait()
    for i in (2, 1, 3):
        send(vcopy(i, False))
    to_major(3)
    to_minor(1)
    to_minor(2)

    for u in (0, 1):
        acc = minor_sum(u)
        for k in range(UNITS[u][2]):
            p3[PLACES[UNITS[u][1] + k]] = acc[k]
    for i in (2, 1, 3):
        send(piece_copy(i, False))
    to_minor(3)
    rows_ref[pl.ds((NX + p) * KW, KW)] = p3[0]
    for i in range(1, NX):
        piece_copy(i, True).wait_recv()
        q = (p + i) % NX
        rows_ref[pl.ds((NX + q) * KW, KW)] = r3[q]
    for u in (2, 3):
        acc = minor_sum(u)
        for k in range(UNITS[u][2]):
            q = (p + PLACES[UNITS[u][1] + k]) % NX
            rows_ref[pl.ds(q * KW, KW)] = acc[k]

    def line(i):
        return peer_at(i // 2, b, c) - c + i % 2

    fetches[7].wait()
    for i in range(16):
        d4[i] = rows_ref[bos_ref[line(i)]]

    def group_copy(i):
        me = c * 8 + a
        return rcopy(d4.at[i], f4.at[me], fs_sem.at[i], fr_sem.at[me], (line(i), p))

    for step in FAR:
        for core in range(2):
            send(group_copy((a + step) % 8 * 2 + core))
    send(group_copy(a * 2 + 1 - c))
    f4[c * 8 + a] = d4[a * 2 + c]

    @pl.loop(1, 16)
    def _(j):
        i = (c * 8 + a + j) % 16
        rcopy(f4.at[i], f4.at[i], fs_sem.at[i], fr_sem.at[i], (sib, p)).wait_recv()

    tiles[0] = f4[...].reshape(BR, BR).astype(BF16)

    def tile_copy(i, land):
        q = (p + i) % NX
        at = i if land else NX - i
        return rcopy(tiles.at[at] if land else tiles.at[0], tiles.at[at], ts_sem.at[i], tr_sem.at[at], (dp, q))

    drain()
    sent.clear()
    for i in (2, 1, 3):
        send(tile_copy(i, False))
    for i in range(1, NX):
        vcopy(i, True).wait_recv()
    fetches[4].wait()
    fetches[8].wait()
    for i in range(1, NX):
        tile_copy(i, True).wait_recv()

    tile = [tiles[i] for i in range(NX)]
    left_sum = None
    stats = []
    for i in range(NX):
        part = lax.dot_general(tile[i], tile[i], (((1,), (1,)), ((), ())), preferred_element_type=F32)
        left_sum = part if left_sum is None else left_sum + part
        gram = lax.dot_general(tile[i], tile[i], (((0,), (0,)), ((), ())), preferred_element_type=F32)
        stats.append(DECAY * rprev[i] + (1.0 - DECAY) * gram)
    stats.append(DECAY * lprev_ref[...] + (1.0 - DECAY) * left_sum)
    roots = [split(r) for r in inverse_fourth_roots(stats)]
    left_root = roots[NX]
    zero = jnp.zeros((BR, BR), BF16)
    mixed = split(mm(left_root, (tile[0], zero)) + mm((tile[0], zero), roots[0]))
    raw = mm(left_root, mixed) + mm(mixed, roots[0])
    squares = raw * raw
    for i in range(1, NX):
        mixed = (bdot(left_root[0], tile[i]) + bdot(tile[i], roots[i][0])).astype(BF16)
        other = bdot(left_root[0], mixed) + bdot(mixed, roots[i][0])
        squares = squares + other * other
    total = jnp.sum(squares, axis=(0, 1), keepdims=True)
    inv = 1.0 / jnp.sqrt(total / (NX * BR * BR) + 1e-6)
    out_ref[...] = jnp.where(cnt_ref[0] > 0, raw * inv, 0.0)

    drain()


def local(
    block_input, block_middle, out_grad, lengths, conv_weight, block_of_slot, slot_count, left_prev, right_prev
):
    vmem = pl.BlockSpec(memory_space=pltpu.VMEM)
    hbm = pl.BlockSpec(memory_space=pltpu.HBM)
    dma = pltpu.SemaphoreType.DMA
    out = pl.pallas_call(
        kernel,
        out_shape=jax.ShapeDtypeStruct((BR, BR), F32),
        in_specs=[hbm] * 9,
        out_specs=vmem,
        scratch_shapes=[
            pltpu.SMEM((NS,), jnp.int32),
            pltpu.SMEM((BR,), jnp.int32),
            pltpu.SMEM((1,), jnp.int32),
            pltpu.VMEM((NS * LEN, BR), BF16),
            pltpu.VMEM((NS * LEN, BR), BF16),
            pltpu.VMEM((NS * LEN, BR), BF16),
            pltpu.VMEM((BR, BR), F32),
            pltpu.VMEM((NX, BR, BR), F32),
            pltpu.VMEM((NX, NS, LEN + 2 * PAD, BR), BF16),
            pltpu.VMEM((NX, NS, BR, LEN), BF16),
            pltpu.VMEM((NS, BR, LEN), BF16),
            pltpu.VMEM((NS * LEN, BR), F32),
            pltpu.VMEM((NX, KW, BR, BR), BF16),
            pltpu.VMEM((NX + 1, NS, LEN, KW * BR), BF16),
            pltpu.VMEM((NS, LEN + 2 * PAD, BR), BF16),
            pltpu.VMEM((2, NX, KW * BR, BR), F32),
            *[pltpu.VMEM((n * KW, 64, BR), F32) for _, _, n in UNITS],
            *[pltpu.VMEM((8, padded_rows(n), BR), BF16) for _, _, n in UNITS],
            *[pltpu.VMEM((8, padded_rows(n), BR), BF16) for _, _, n in UNITS],
            *[pltpu.VMEM((padded_rows(n), BR), BF16) for _, _, n in UNITS],
            *[pltpu.VMEM((8, padded_rows(n), BR), BF16) for _, _, n in UNITS],
            pltpu.VMEM((NX, KW, 8, BR), F32),
            pltpu.VMEM((NX, KW, 8, BR), F32),
            pltpu.VMEM((2 * NX * KW, 8, BR), F32),
            pltpu.VMEM((16, 8, BR), F32),
            pltpu.VMEM((16, 8, BR), F32),
            pltpu.VMEM((NX, BR, BR), BF16),
            dma((6,)), dma((6,)), dma((6,)), dma((6,)), dma((NX,)), dma((NX,)), dma((8,)), dma((8,)), dma((8,)),
            dma((4, 8)), dma((4, 8)), dma((4, 8)), dma((4, 8)), dma((NX,)), dma((NX,)),
            dma((16,)), dma((16,)), dma((NX,)), dma((NX,)), dma((NX,)), dma((NX,)), dma((9,)),
        ],
        compiler_params=pltpu.CompilerParams(
            collective_id=0, has_side_effects=True, vmem_limit_bytes=60 * 1024 * 1024
        ),
    )(
        block_input, block_middle, out_grad, lengths, conv_weight.transpose(1, 0, 2), block_of_slot,
        slot_count, left_prev.reshape(BR, BR), right_prev.reshape(BR, BR),
    )
    return out.reshape(1, BR * BR)


def solution(mesh):
    return jax.shard_map(
        local,
        mesh=mesh,
        in_specs=(
            P("dp", "owner"), P("dp", "owner"), P("dp", "owner"), P("dp"), P(None, None, "owner"), P(),
            P("dp"), P("dp", None), P("dp", "owner"),
        ),
        out_specs=P("dp", "owner"),
        check_vma=False,
    )
```

```python
import jax
import jax.numpy as jnp
from jax import lax
from jax.experimental import pallas as pl
from jax.experimental.pallas import tpu as pltpu
from jax.sharding import PartitionSpec as P

MESH = pl.DeviceIdType.MESH
F32, BF16 = jnp.float32, jnp.bfloat16
KW = 5
BR = 128
LEN = 512
PAD = 16
NS = 2
NX, NY, NZ = 4, 8, 8
ITERS = 8
DECAY = 0.9


def split(a):
    high = a.astype(BF16)
    return high, (a - high.astype(F32)).astype(BF16)


def mm(a, b):
    (ah, al), (bh, bl) = a, b
    left = jnp.concatenate([ah, al], axis=1)
    right = jnp.concatenate(
        [jnp.concatenate([bh, bl], axis=1), jnp.concatenate([bh, jnp.zeros_like(bl)], axis=1)], axis=0
    )
    both = jnp.dot(left, right, preferred_element_type=F32)
    return both[:, :BR] + both[:, BR:]


def bdot(a, b):
    return jnp.dot(a, b, preferred_element_type=F32)


def inverse_fourth_roots(stats):
    rows = lax.broadcasted_iota(jnp.int32, (BR, BR), 0)
    cols = lax.broadcasted_iota(jnp.int32, (BR, BR), 1)
    eye = (rows == cols).astype(F32)
    norms = [jnp.sqrt(jnp.sum(s * s, axis=(0, 1), keepdims=True)) for s in stats]
    cur = [s / n for s, n in zip(stats, norms)]
    root = None
    for it in range(ITERS):
        fac = [1.25 * eye - 0.25 * m for m in cur]
        parts = [split(f) for f in fac]
        if it < ITERS - 1:
            square = [split(mm(f, f)) for f in parts]
            half = [split(mm(s, split(m))) for s, m in zip(square, cur)]
            cur = [mm(h, s) for h, s in zip(half, square)]
        root = fac if it == 0 else [mm(split(r), f) for r, f in zip(root, parts)]
    scale = [1.0 / jnp.sqrt(jnp.sqrt(n)) for n in norms]
    return [r * s for r, s in zip(root, scale)]


def peer_at(major, minor, core):
    z = major + core * (minor - major)
    y = minor + core * (major - minor)
    return (z * NY + y) * 2 + core


PLACES = (0, 3, 1, 2)
UNITS = ((1, 0, 3), (1, 3, 1), (0, 0, 3), (0, 3, 1))
FAR = (4, 3, 5, 2, 6, 1, 7)


def padded_rows(places):
    return -(-places * KW * 8 // 16) * 16


def kernel(
    x1_hbm, x2_hbm, g_hbm, len_hbm, w_ref, bos_hbm, cnt_hbm, lprev_hbm, rprev_hbm, out_ref,
    len_ref, bos_ref, cnt_ref, x1_ref, x2_ref, g_ref, lprev_ref, rprev,
    gbuf, hbuf, h2t, slope, wbuf, gst, g1, kbuf,
    c0, c1, c2, c3, pa0, pa1, pa2, pa3, ra0, ra1, ra2, ra3, pb0, pb1, pb2, pb3, rb0, rb1, rb2, rb3, p3, r3, rows_ref, d4, f4, tiles,
    gs_sem, gr_sem, hs_sem, hr_sem, ws_sem, wr_sem, as_sem, ar_sem, c0_sem, s1_sem, r1_sem, s2_sem, r2_sem,
    s3_sem, r3_sem, fs_sem, fr_sem, vs_sem, vr_sem, ts_sem, tr_sem, in_sem, word_sem,
):
    dp, p = lax.axis_index("dp"), lax.axis_index("owner")
    c = dp % 2
    y = (dp // 2) % NY
    z = dp // (2 * NY)
    a = z + c * (y - z)
    b = y + c * (z - y)
    right, left = (p + 1) % NX, (p + 3) % NX
    core_in, pa, ra = (c0, c1, c2, c3), (pa0, pa1, pa2, pa3), (ra0, ra1, ra2, ra3)
    pb, rb = (pb0, pb1, pb2, pb3), (rb0, rb1, rb2, rb3)

    barrier = pltpu.get_barrier_semaphore()

    def greet(dev):
        pl.semaphore_signal(barrier, inc=1, device_id=dev, device_id_type=MESH)

    near = [((z * NY + (y + step) % NY) * 2 + c, p) for step in (1, 7)]
    near += [((((z + step) % NZ) * NY + y) * 2 + c, p) for step in (1, 7)]
    for dev in near:
        greet(dev)
    for step in (2, 1, 3):
        greet((dp, (p + step) % NX))
    greet((dp + 1 - 2 * c, p))

    def tell(k):
        for dev in near:
            pl.semaphore_signal(word_sem.at[k], inc=1, device_id=dev, device_id_type=MESH)

    def heard(k):
        pl.semaphore_wait(word_sem.at[k], 4)

    def rcopy(src, dst, ss, rs, dev):
        return pltpu.make_async_remote_copy(
            src_ref=src, dst_ref=dst, send_sem=ss, recv_sem=rs, device_id=dev, device_id_type=MESH
        )

    def fetch(i, src, dst):
        return pltpu.make_async_copy(src, dst, in_sem.at[i])

    own = pl.ds(pl.multiple_of(p * BR, BR), BR)
    fetches = [
        fetch(0, g_hbm, g_ref), fetch(1, x1_hbm, x1_ref), fetch(2, x2_hbm, x2_ref),
        fetch(3, w_ref.at[:, own, :], wbuf.at[0]), fetch(4, lprev_hbm, lprev_ref), fetch(5, rprev_hbm, rprev.at[0]),
        fetch(6, len_hbm, len_ref), fetch(7, bos_hbm, bos_ref), fetch(8, cnt_hbm, cnt_ref),
    ]
    for i in (6, 0, 1, 2, 3, 4, 5, 7, 8):
        fetches[i].start()

    sent = []

    def send(copy):
        copy.start()
        sent.append(copy)

    def drain():
        for copy in sent:
            copy.wait_send()

    zpad = jnp.zeros((PAD, BR), BF16)
    for slot in range(NX):
        for s in range(NS):
            gbuf[slot, s, 0:PAD, :] = zpad
            gbuf[slot, s, PAD + LEN : PAD + LEN + PAD, :] = zpad
    for s in range(NS):
        g1[s, 0:PAD, :] = zpad
        g1[s, PAD + LEN : PAD + LEN + PAD, :] = zpad
    tok = lax.broadcasted_iota(jnp.int32, (LEN, BR), 0)
    fetches[6].wait()
    fetches[0].wait()
    for s in range(NS):
        v = g_ref[s * LEN : (s + 1) * LEN, :].astype(F32)
        gbuf[0, s, PAD : PAD + LEN, :] = jnp.where(tok < len_ref[s], v, 0.0).astype(BF16)

    pl.semaphore_wait(barrier, 4 + 3 + 1)

    def gpiece(slot, s):
        return gbuf.at[slot, s, pl.ds(PAD, LEN), :]

    def hpiece(slot, s):
        return hbuf.at[slot, s]

    plan = [
        (0, 3, 1, right), (0, 3, 0, right), (0, 1, 0, left), (0, 1, 1, left),
        (1, 2, 0, left), (3, 2, 1, right),
    ]

    def xcopy(piece, ss, rs, i):
        src, dst, s, dev = plan[i]
        return rcopy(piece(src, s), piece(dst, s), ss.at[i], rs.at[i], (dp, dev))

    def xland(piece, ss, rs, i):
        src, dst, s, dev = plan[i]
        rcopy(piece(dst, s), piece(dst, s), ss.at[i], rs.at[i], (dp, dev)).wait_recv()

    def wcopy(i):
        q = (p + i) % NX
        src = w_ref.at[:, pl.ds(pl.multiple_of(q * BR + a * 16, 16), 16), :]
        dst = wbuf.at[NX - i, :, pl.ds(pl.multiple_of(a * 16, 16), 16), :]
        return rcopy(src, dst, ws_sem.at[NX - i], wr_sem.at[NX - i], (dp, q))

    def wpart(t):
        return wbuf.at[pl.ds(1, NX - 1), :, pl.ds(pl.multiple_of(t * 16, 16), 16), :]

    def wspread(i):
        t = (a + i) % 8
        return rcopy(wpart(a), wpart(a), as_sem.at[t], ar_sem.at[a], (peer_at(t, b, c), p))

    def wspread_land(i):
        t = (a + i) % 8
        rcopy(wpart(t), wpart(t), as_sem.at[t], ar_sem.at[t], (peer_at(t, b, c), p)).wait_recv()

    for i in (2, 1, 3):
        send(wcopy(i))
    for i in (0, 2, 1, 3):
        send(xcopy(gpiece, gs_sem, gr_sem, i))

    tell(0)

    fetches[1].wait()

    @pl.loop(0, NS * LEN // BR)
    def _(i):
        s = i // (LEN // BR)
        t0 = pl.multiple_of((i % (LEN // BR)) * BR, BR)
        r0 = pl.multiple_of(i * BR, BR)
        valid = (lax.broadcasted_iota(jnp.int32, (BR, BR), 0) + t0 < len_ref[s]).astype(F32)
        x = x1_ref[pl.ds(r0, BR), :].astype(F32)
        h = x * (0.5 * (1.0 + lax.erf(x * 0.7071067811865476))) * valid
        hbuf[0, s, :, pl.ds(t0, BR)] = h.T.astype(BF16)

    heard(0)
    tell(1)
    fetches[2].wait()

    @pl.loop(0, NS * LEN // BR)
    def _(i):
        s = i // (LEN // BR)
        t0 = pl.multiple_of((i % (LEN // BR)) * BR, BR)
        r0 = pl.multiple_of(i * BR, BR)
        valid = (lax.broadcasted_iota(jnp.int32, (BR, BR), 0) + t0 < len_ref[s]).astype(F32)
        x = x2_ref[pl.ds(r0, BR), :].astype(F32)
        phi = 0.5 * (1.0 + lax.erf(x * 0.7071067811865476))
        h2t[s, :, pl.ds(t0, BR)] = (x * phi * valid).T.astype(BF16)
        slope[pl.ds(r0, BR), :] = (phi + x * jnp.exp(-0.5 * x * x) * 0.3989422804014327) * valid

    def stack(src, slot, dilation):
        for s in range(NS):
            for k in range(KW):
                r0 = PAD - (k - KW // 2) * dilation
                gst[slot, s, :, k * BR : (k + 1) * BR] = src[s, r0 : r0 + LEN, :]

    def put_piece(kk, place, acts, slot):
        prod = jnp.dot(acts[0], gst[slot, 0], preferred_element_type=F32)
        prod += jnp.dot(acts[1], gst[slot, 1], preferred_element_type=F32)
        for k in range(KW):
            kbuf[kk, place, pl.ds(k, BR, stride=KW), :] = prod[:, k * BR : (k + 1) * BR]

    def second_piece(place):
        stack(gbuf.at[PLACES[place]], PLACES[place], 8)
        put_piece(1, place, h2t, PLACES[place])

    sib = dp + 1 - 2 * c

    def ktile(u):
        kk, first, places = UNITS[u]
        return kbuf.at[kk].reshape(NX * KW, BR, BR).at[pl.ds(first * KW, places * KW)]

    def core_copy(u):
        other = pl.ds(pl.multiple_of((1 - c) * 64, 64), 64)
        return rcopy(
            ktile(u).at[:, other, :], core_in[u], c0_sem.at[2 * u], c0_sem.at[2 * u + 1], (sib, p)
        )

    def major_copy(u, t, land):
        return rcopy(
            ra[u].at[t] if land else pa[u].at[t], ra[u].at[t if land else a],
            s1_sem.at[u, t], r1_sem.at[u, t if land else a], (peer_at(t, b, c), p),
        )

    def minor_copy(u, t, land):
        return rcopy(
            rb[u].at[t] if land else pb[u], rb[u].at[t if land else b],
            s2_sem.at[u, t], r2_sem.at[u, t if land else b], (peer_at(a, t, c), p),
        )

    def to_major(u):
        core_copy(u).wait_recv()
        rows = UNITS[u][2] * KW * 8
        mine = pl.multiple_of(c * 64, 64)

        def fill(t):
            t8 = pl.multiple_of(t * 8, 8)
            both = ktile(u)[:, pl.ds(mine + t8, 8), :] + core_in[u][:, pl.ds(t8, 8), :]
            both = both.reshape(rows, BR)
            if padded_rows(UNITS[u][2]) > rows:
                both = jnp.concatenate([both, jnp.zeros((8, BR), F32)], axis=0)
            pa[u][t] = both.astype(BF16)

        for step in FAR:
            t = (a + step) % 8
            fill(t)
            send(major_copy(u, t, False))
        fill(a)

    def to_minor(u):
        acc = pa[u][a].astype(F32)
        for i in range(1, 8):
            t = (a + i) % 8
            major_copy(u, t, True).wait_recv()
            acc = acc + ra[u][t].astype(F32)
        pb[u][...] = acc.astype(BF16)

        for step in FAR:
            send(minor_copy(u, (b + step) % 8, False))

    def minor_sum(u):
        acc = pb[u][...].astype(F32)
        for i in range(1, 8):
            t = (b + i) % 8
            minor_copy(u, t, True).wait_recv()
            acc = acc + rb[u][t].astype(F32)
        places = UNITS[u][2]
        return acc[: places * KW * 8].reshape(places, KW, 8, BR)

    def vcopy(i, land):
        q = (p + i) % NX
        at = i if land else NX - i
        return rcopy(rprev.at[at] if land else rprev.at[0], rprev.at[at], vs_sem.at[i], vr_sem.at[at], (dp, q))

    def piece_copy(i, land):
        q = (p + i) % NX
        return rcopy(
            r3.at[q] if land else p3.at[i], r3.at[q if land else p],
            s3_sem.at[i], r3_sem.at[q if land else p], (dp, q),
        )


    def first_piece(place):
        put_piece(0, place, hbuf.at[PLACES[place]], NX)

    def cotangent(s):
        back = None
        for slot in range(NX):
            wcat = jnp.concatenate([wbuf[slot, k] for k in range(KW)], axis=1)
            part = lax.dot_general(gst[slot, s], wcat, (((1,), (1,)), ((), ())), preferred_element_type=F32)
            back = part if back is None else back + part
        g1[s, PAD : PAD + LEN, :] = (
            gbuf[0, s, PAD : PAD + LEN, :].astype(F32) + slope[s * LEN : (s + 1) * LEN, :] * back
        ).astype(BF16)

    heard(1)
    tell(2)
    second_piece(0)
    for i in range(1, NX):
        wcopy(i).wait_recv()
    heard(2)
    for step in FAR:
        send(wspread(step))
    xland(gpiece, gs_sem, gr_sem, 0)
    send(xcopy(gpiece, gs_sem, gr_sem, 5))
    xland(gpiece, gs_sem, gr_sem, 2)
    send(xcopy(gpiece, gs_sem, gr_sem, 4))
    xland(gpiece, gs_sem, gr_sem, 1)
    xland(gpiece, gs_sem, gr_sem, 3)
    for i in (0, 2, 1, 3):
        send(xcopy(hpiece, hs_sem, hr_sem, i))
    second_piece(1)
    second_piece(2)
    send(core_copy(0))
    xland(gpiece, gs_sem, gr_sem, 4)
    xland(gpiece, gs_sem, gr_sem, 5)
    second_piece(3)
    send(core_copy(1))
    to_major(0)
    @pl.loop(1, 8)
    def _(i):
        wspread_land(i)

    fetches[3].wait()
    cotangent(0)
    to_major(1)
    cotangent(1)
    stack(g1, NX, 4)
    first_piece(0)
    xland(hpiece, hs_sem, hr_sem, 0)
    send(xcopy(hpiece, hs_sem, hr_sem, 5))
    xland(hpiece, hs_sem, hr_sem, 2)
    send(xcopy(hpiece, hs_sem, hr_sem, 4))
    xland(hpiece, hs_sem, hr_sem, 1)
    first_piece(1)
    xland(hpiece, hs_sem, hr_sem, 3)
    first_piece(2)
    send(core_copy(2))
    to_minor(0)
    to_major(2)
    xland(hpiece, hs_sem, hr_sem, 4)
    xland(hpiece, hs_sem, hr_sem, 5)
    first_piece(3)
    send(core_copy(3))
    fetches[5].wait()
    for i in (2, 1, 3):
        send(vcopy(i, False))
    to_major(3)
    to_minor(1)
    to_minor(2)
    to_minor(3)
    for u in (0, 1):
        acc = minor_sum(u)
        for k in range(UNITS[u][2]):
            p3[PLACES[UNITS[u][1] + k]] = acc[k]
    for i in (2, 1, 3):
        send(piece_copy(i, False))
    rows_ref[pl.ds((NX + p) * KW, KW)] = p3[0]
    for i in range(1, NX):
        piece_copy(i, True).wait_recv()
        q = (p + i) % NX
        rows_ref[pl.ds((NX + q) * KW, KW)] = r3[q]
    for u in (2, 3):
        acc = minor_sum(u)
        for k in range(UNITS[u][2]):
            q = (p + PLACES[UNITS[u][1] + k]) % NX
            rows_ref[pl.ds(q * KW, KW)] = acc[k]

    def line(i):
        return peer_at(i // 2, b, c) - c + i % 2

    fetches[7].wait()
    for i in range(16):
        d4[i] = rows_ref[bos_ref[line(i)]]

    def group_copy(i):
        me = c * 8 + a
        return rcopy(d4.at[i], f4.at[me], fs_sem.at[i], fr_sem.at[me], (line(i), p))

    for step in FAR:
        for core in range(2):
            send(group_copy((a + step) % 8 * 2 + core))
    send(group_copy(a * 2 + 1 - c))
    f4[c * 8 + a] = d4[a * 2 + c]

    @pl.loop(1, 16)
    def _(j):
        i = (c * 8 + a + j) % 16
        rcopy(f4.at[i], f4.at[i], fs_sem.at[i], fr_sem.at[i], (sib, p)).wait_recv()

    tiles[0] = f4[...].reshape(BR, BR).astype(BF16)

    def tile_copy(i, land):
        q = (p + i) % NX
        at = i if land else NX - i
        return rcopy(tiles.at[at] if land else tiles.at[0], tiles.at[at], ts_sem.at[i], tr_sem.at[at], (dp, q))

    drain()
    sent.clear()
    for i in (2, 1, 3):
        send(tile_copy(i, False))
    for i in range(1, NX):
        vcopy(i, True).wait_recv()
    fetches[4].wait()
    fetches[8].wait()
    for i in range(1, NX):
        tile_copy(i, True).wait_recv()

    tile = [tiles[i] for i in range(NX)]
    left_sum = None
    stats = []
    for i in range(NX):
        part = lax.dot_general(tile[i], tile[i], (((1,), (1,)), ((), ())), preferred_element_type=F32)
        left_sum = part if left_sum is None else left_sum + part
        gram = lax.dot_general(tile[i], tile[i], (((0,), (0,)), ((), ())), preferred_element_type=F32)
        stats.append(DECAY * rprev[i] + (1.0 - DECAY) * gram)
    stats.append(DECAY * lprev_ref[...] + (1.0 - DECAY) * left_sum)
    roots = [split(r) for r in inverse_fourth_roots(stats)]
    left_root = roots[NX]
    zero = jnp.zeros((BR, BR), BF16)
    mixed = split(mm(left_root, (tile[0], zero)) + mm((tile[0], zero), roots[0]))
    raw = mm(left_root, mixed) + mm(mixed, roots[0])
    squares = raw * raw
    for i in range(1, NX):
        mixed = (bdot(left_root[0], tile[i]) + bdot(tile[i], roots[i][0])).astype(BF16)
        other = bdot(left_root[0], mixed) + bdot(mixed, roots[i][0])
        squares = squares + other * other
    total = jnp.sum(squares, axis=(0, 1), keepdims=True)
    inv = 1.0 / jnp.sqrt(total / (NX * BR * BR) + 1e-6)
    out_ref[...] = jnp.where(cnt_ref[0] > 0, raw * inv, 0.0)

    drain()


def local(
    block_input, block_middle, out_grad, lengths, conv_weight, block_of_slot, slot_count, left_prev, right_prev
):
    vmem = pl.BlockSpec(memory_space=pltpu.VMEM)
    hbm = pl.BlockSpec(memory_space=pltpu.HBM)
    dma = pltpu.SemaphoreType.DMA
    out = pl.pallas_call(
        kernel,
        out_shape=jax.ShapeDtypeStruct((BR, BR), F32),
        in_specs=[hbm] * 9,
        out_specs=vmem,
        scratch_shapes=[
            pltpu.SMEM((NS,), jnp.int32),
            pltpu.SMEM((BR,), jnp.int32),
            pltpu.SMEM((1,), jnp.int32),
            pltpu.VMEM((NS * LEN, BR), BF16),
            pltpu.VMEM((NS * LEN, BR), BF16),
            pltpu.VMEM((NS * LEN, BR), BF16),
            pltpu.VMEM((BR, BR), F32),
            pltpu.VMEM((NX, BR, BR), F32),
            pltpu.VMEM((NX, NS, LEN + 2 * PAD, BR), BF16),
            pltpu.VMEM((NX, NS, BR, LEN), BF16),
            pltpu.VMEM((NS, BR, LEN), BF16),
            pltpu.VMEM((NS * LEN, BR), F32),
            pltpu.VMEM((NX, KW, BR, BR), BF16),
            pltpu.VMEM((NX + 1, NS, LEN, KW * BR), BF16),
            pltpu.VMEM((NS, LEN + 2 * PAD, BR), BF16),
            pltpu.VMEM((2, NX, KW * BR, BR), F32),
            *[pltpu.VMEM((n * KW, 64, BR), F32) for _, _, n in UNITS],
            *[pltpu.VMEM((8, padded_rows(n), BR), BF16) for _, _, n in UNITS],
            *[pltpu.VMEM((8, padded_rows(n), BR), BF16) for _, _, n in UNITS],
            *[pltpu.VMEM((padded_rows(n), BR), BF16) for _, _, n in UNITS],
            *[pltpu.VMEM((8, padded_rows(n), BR), BF16) for _, _, n in UNITS],
            pltpu.VMEM((NX, KW, 8, BR), F32),
            pltpu.VMEM((NX, KW, 8, BR), F32),
            pltpu.VMEM((2 * NX * KW, 8, BR), F32),
            pltpu.VMEM((16, 8, BR), F32),
            pltpu.VMEM((16, 8, BR), F32),
            pltpu.VMEM((NX, BR, BR), BF16),
            dma((6,)), dma((6,)), dma((6,)), dma((6,)), dma((NX,)), dma((NX,)), dma((8,)), dma((8,)), dma((8,)),
            dma((4, 8)), dma((4, 8)), dma((4, 8)), dma((4, 8)), dma((NX,)), dma((NX,)),
            dma((16,)), dma((16,)), dma((NX,)), dma((NX,)), dma((NX,)), dma((NX,)), dma((9,)),
            pltpu.SemaphoreType.REGULAR((3,)),
        ],
        compiler_params=pltpu.CompilerParams(
            collective_id=0, has_side_effects=True, vmem_limit_bytes=60 * 1024 * 1024
        ),
    )(
        block_input, block_middle, out_grad, lengths, conv_weight.transpose(1, 0, 2), block_of_slot,
        slot_count, left_prev.reshape(BR, BR), right_prev.reshape(BR, BR),
    )
    return out.reshape(1, BR * BR)


def solution(mesh):
    return jax.shard_map(
        local,
        mesh=mesh,
        in_specs=(
            P("dp", "owner"), P("dp", "owner"), P("dp", "owner"), P("dp"), P(None, None, "owner"), P(),
            P("dp"), P("dp", None), P("dp", "owner"),
        ),
        out_specs=P("dp", "owner"),
        check_vma=False,
    )
```

```python
import jax
import jax.numpy as jnp
from jax import lax
from jax.experimental import pallas as pl
from jax.experimental.pallas import tpu as pltpu
from jax.sharding import PartitionSpec as P

MESH = pl.DeviceIdType.MESH
F32, BF16 = jnp.float32, jnp.bfloat16
KW = 5
BR = 128
LEN = 512
PAD = 16
NS = 2
NX, NY, NZ = 4, 8, 8
ITERS = 8
DECAY = 0.9


def split(a):
    high = a.astype(BF16)
    return high, (a - high.astype(F32)).astype(BF16)


def mm(a, b):
    (ah, al), (bh, bl) = a, b
    left = jnp.concatenate([ah, al], axis=1)
    right = jnp.concatenate(
        [jnp.concatenate([bh, bl], axis=1), jnp.concatenate([bh, jnp.zeros_like(bl)], axis=1)], axis=0
    )
    both = jnp.dot(left, right, preferred_element_type=F32)
    return both[:, :BR] + both[:, BR:]


def bdot(a, b):
    return jnp.dot(a, b, preferred_element_type=F32)


def inverse_fourth_roots(stats):
    rows = lax.broadcasted_iota(jnp.int32, (BR, BR), 0)
    cols = lax.broadcasted_iota(jnp.int32, (BR, BR), 1)
    eye = (rows == cols).astype(F32)
    norms = [jnp.sqrt(jnp.sum(s * s, axis=(0, 1), keepdims=True)) for s in stats]
    cur = [s / n for s, n in zip(stats, norms)]
    root = None
    for it in range(ITERS):
        fac = [1.25 * eye - 0.25 * m for m in cur]
        parts = [split(f) for f in fac]
        if it < ITERS - 1:
            square = [split(mm(f, f)) for f in parts]
            half = [split(mm(s, split(m))) for s, m in zip(square, cur)]
            cur = [mm(h, s) for h, s in zip(half, square)]
        root = fac if it == 0 else [mm(split(r), f) for r, f in zip(root, parts)]
    scale = [1.0 / jnp.sqrt(jnp.sqrt(n)) for n in norms]
    return [r * s for r, s in zip(root, scale)]


def peer_at(major, minor, core):
    z = major + core * (minor - major)
    y = minor + core * (major - minor)
    return (z * NY + y) * 2 + core


PLACES = (0, 3, 1, 2)
UNITS = ((1, 0, 3), (1, 3, 1), (0, 0, 3), (0, 3, 1))
FAR = (4, 3, 5, 2, 6, 1, 7)


def padded_rows(places):
    return -(-places * KW * 8 // 16) * 16


def kernel(
    x1_hbm, x2_hbm, g_hbm, len_hbm, w_ref, bos_hbm, cnt_hbm, lprev_hbm, rprev_hbm, out_ref,
    len_ref, bos_ref, cnt_ref, x1_ref, x2_ref, g_ref, lprev_ref, rprev,
    gbuf, hbuf, h2t, slope, wbuf, gst, g1, kbuf,
    c0, c1, c2, c3, pa0, pa1, pa2, pa3, ra0, ra1, ra2, ra3, pb0, pb1, pb2, pb3, rb0, rb1, rb2, rb3, p3, r3, rows_ref, d4, f4, tiles,
    gs_sem, gr_sem, hs_sem, hr_sem, ws_sem, wr_sem, as_sem, ar_sem, c0_sem, s1_sem, r1_sem, s2_sem, r2_sem,
    s3_sem, r3_sem, fs_sem, fr_sem, vs_sem, vr_sem, ts_sem, tr_sem, in_sem, word_sem,
):
    dp, p = lax.axis_index("dp"), lax.axis_index("owner")
    c = dp % 2
    right, left = (p + 1) % NX, (p + 3) % NX
    y = (dp // 2) % NY
    z = dp // (2 * NY)
    a = z + c * (y - z)
    b = y + c * (z - y)
    core_in, pa, ra = (c0, c1, c2, c3), (pa0, pa1, pa2, pa3), (ra0, ra1, ra2, ra3)
    pb, rb = (pb0, pb1, pb2, pb3), (rb0, rb1, rb2, rb3)

    barrier = pltpu.get_barrier_semaphore()

    def greet(dev):
        pl.semaphore_signal(barrier, inc=1, device_id=dev, device_id_type=MESH)

    near = [((z * NY + (y + step) % NY) * 2 + c, p) for step in (1, 7)]
    near += [((((z + step) % NZ) * NY + y) * 2 + c, p) for step in (1, 7)]
    near += [(dp, right), (dp, left)]
    for dev in near:
        greet(dev)
    greet((dp + 1 - 2 * c, p))

    def tell(k):
        for dev in near:
            pl.semaphore_signal(word_sem.at[k], inc=1, device_id=dev, device_id_type=MESH)

    def heard(k):
        pl.semaphore_wait(word_sem.at[k], 6)

    def rcopy(src, dst, ss, rs, dev):
        return pltpu.make_async_remote_copy(
            src_ref=src, dst_ref=dst, send_sem=ss, recv_sem=rs, device_id=dev, device_id_type=MESH
        )

    def fetch(i, src, dst):
        return pltpu.make_async_copy(src, dst, in_sem.at[i])

    own = pl.ds(pl.multiple_of(p * BR, BR), BR)
    fetches = [
        fetch(0, g_hbm, g_ref), fetch(1, x1_hbm, x1_ref), fetch(2, x2_hbm, x2_ref),
        fetch(3, w_ref.at[:, own, :], wbuf.at[0]), fetch(4, lprev_hbm, lprev_ref), fetch(5, rprev_hbm, rprev.at[0]),
        fetch(6, len_hbm, len_ref), fetch(7, bos_hbm, bos_ref), fetch(8, cnt_hbm, cnt_ref),
    ]
    for i in (6, 0, 1, 2, 3, 4, 5, 7, 8):
        fetches[i].start()

    sent = []

    def send(copy):
        copy.start()
        sent.append(copy)

    def drain():
        for copy in sent:
            copy.wait_send()

    zpad = jnp.zeros((PAD, BR), BF16)
    for slot in range(NX):
        for s in range(NS):
            gbuf[slot, s, 0:PAD, :] = zpad
            gbuf[slot, s, PAD + LEN : PAD + LEN + PAD, :] = zpad
    for s in range(NS):
        g1[s, 0:PAD, :] = zpad
        g1[s, PAD + LEN : PAD + LEN + PAD, :] = zpad
    tok = lax.broadcasted_iota(jnp.int32, (LEN, BR), 0)
    fetches[6].wait()
    fetches[0].wait()
    for s in range(NS):
        v = g_ref[s * LEN : (s + 1) * LEN, :].astype(F32)
        gbuf[0, s, PAD : PAD + LEN, :] = jnp.where(tok < len_ref[s], v, 0.0).astype(BF16)

    pl.semaphore_wait(barrier, 4 + 2 + 1)

    def gpiece(slot, s):
        return gbuf.at[slot, s, pl.ds(PAD, LEN), :]

    def hpiece(slot, s):
        return hbuf.at[slot, s]

    plan = [
        (0, 3, 1, right), (0, 3, 0, right), (0, 1, 0, left), (0, 1, 1, left),
        (1, 2, 0, left), (3, 2, 1, right),
    ]

    def xcopy(piece, ss, rs, i):
        src, dst, s, dev = plan[i]
        return rcopy(piece(src, s), piece(dst, s), ss.at[i], rs.at[i], (dp, dev))

    def xland(piece, ss, rs, i):
        src, dst, s, dev = plan[i]
        rcopy(piece(dst, s), piece(dst, s), ss.at[i], rs.at[i], (dp, dev)).wait_recv()

    def wcopy(i):
        q = (p + i) % NX
        src = w_ref.at[:, pl.ds(pl.multiple_of(q * BR + a * 16, 16), 16), :]
        dst = wbuf.at[NX - i, :, pl.ds(pl.multiple_of(a * 16, 16), 16), :]
        return rcopy(src, dst, ws_sem.at[NX - i], wr_sem.at[NX - i], (dp, q))

    def wpart(t):
        return wbuf.at[pl.ds(1, NX - 1), :, pl.ds(pl.multiple_of(t * 16, 16), 16), :]

    def wspread(i):
        t = (a + i) % 8
        return rcopy(wpart(a), wpart(a), as_sem.at[t], ar_sem.at[a], (peer_at(t, b, c), p))

    def wspread_land(i):
        t = (a + i) % 8
        rcopy(wpart(t), wpart(t), as_sem.at[t], ar_sem.at[t], (peer_at(t, b, c), p)).wait_recv()

    for i in (1, 3):
        send(wcopy(i))
    for i in (0, 2):
        send(xcopy(gpiece, gs_sem, gr_sem, i))

    tell(0)

    fetches[1].wait()

    @pl.loop(0, NS * LEN // BR)
    def _(i):
        s = i // (LEN // BR)
        t0 = pl.multiple_of((i % (LEN // BR)) * BR, BR)
        r0 = pl.multiple_of(i * BR, BR)
        valid = (lax.broadcasted_iota(jnp.int32, (BR, BR), 0) + t0 < len_ref[s]).astype(F32)
        x = x1_ref[pl.ds(r0, BR), :].astype(F32)
        h = x * (0.5 * (1.0 + lax.erf(x * 0.7071067811865476))) * valid
        hbuf[0, s, :, pl.ds(t0, BR)] = h.T.astype(BF16)

    heard(0)
    send(wcopy(2))
    for i in (1, 3):
        send(xcopy(gpiece, gs_sem, gr_sem, i))
    tell(1)
    fetches[2].wait()

    @pl.loop(0, NS * LEN // BR)
    def _(i):
        s = i // (LEN // BR)
        t0 = pl.multiple_of((i % (LEN // BR)) * BR, BR)
        r0 = pl.multiple_of(i * BR, BR)
        valid = (lax.broadcasted_iota(jnp.int32, (BR, BR), 0) + t0 < len_ref[s]).astype(F32)
        x = x2_ref[pl.ds(r0, BR), :].astype(F32)
        phi = 0.5 * (1.0 + lax.erf(x * 0.7071067811865476))
        h2t[s, :, pl.ds(t0, BR)] = (x * phi * valid).T.astype(BF16)
        slope[pl.ds(r0, BR), :] = (phi + x * jnp.exp(-0.5 * x * x) * 0.3989422804014327) * valid

    def stack(src, slot, dilation):
        for s in range(NS):
            for k in range(KW):
                r0 = PAD - (k - KW // 2) * dilation
                gst[slot, s, :, k * BR : (k + 1) * BR] = src[s, r0 : r0 + LEN, :]

    def put_piece(kk, place, acts, slot):
        prod = jnp.dot(acts[0], gst[slot, 0], preferred_element_type=F32)
        prod += jnp.dot(acts[1], gst[slot, 1], preferred_element_type=F32)
        for k in range(KW):
            kbuf[kk, place, pl.ds(k, BR, stride=KW), :] = prod[:, k * BR : (k + 1) * BR]

    def second_piece(place):
        stack(gbuf.at[PLACES[place]], PLACES[place], 8)
        put_piece(1, place, h2t, PLACES[place])

    sib = dp + 1 - 2 * c

    def ktile(u):
        kk, first, places = UNITS[u]
        return kbuf.at[kk].reshape(NX * KW, BR, BR).at[pl.ds(first * KW, places * KW)]

    def core_copy(u):
        other = pl.ds(pl.multiple_of((1 - c) * 64, 64), 64)
        return rcopy(
            ktile(u).at[:, other, :], core_in[u], c0_sem.at[2 * u], c0_sem.at[2 * u + 1], (sib, p)
        )

    def major_copy(u, t, land):
        return rcopy(
            ra[u].at[t] if land else pa[u].at[t], ra[u].at[t if land else a],
            s1_sem.at[u, t], r1_sem.at[u, t if land else a], (peer_at(t, b, c), p),
        )

    def minor_copy(u, t, land):
        return rcopy(
            rb[u].at[t] if land else pb[u], rb[u].at[t if land else b],
            s2_sem.at[u, t], r2_sem.at[u, t if land else b], (peer_at(a, t, c), p),
        )

    def to_major(u):
        core_copy(u).wait_recv()
        rows = UNITS[u][2] * KW * 8
        mine = pl.multiple_of(c * 64, 64)

        def fill(t):
            t8 = pl.multiple_of(t * 8, 8)
            both = ktile(u)[:, pl.ds(mine + t8, 8), :] + core_in[u][:, pl.ds(t8, 8), :]
            both = both.reshape(rows, BR)
            if padded_rows(UNITS[u][2]) > rows:
                both = jnp.concatenate([both, jnp.zeros((8, BR), F32)], axis=0)
            pa[u][t] = both.astype(BF16)

        for step in FAR:
            t = (a + step) % 8
            fill(t)
            send(major_copy(u, t, False))
        fill(a)

    def to_minor(u):
        acc = pa[u][a].astype(F32)
        for i in range(1, 8):
            t = (a + i) % 8
            major_copy(u, t, True).wait_recv()
            acc = acc + ra[u][t].astype(F32)
        pb[u][...] = acc.astype(BF16)

        for step in FAR:
            send(minor_copy(u, (b + step) % 8, False))

    def minor_sum(u):
        acc = pb[u][...].astype(F32)
        for i in range(1, 8):
            t = (b + i) % 8
            minor_copy(u, t, True).wait_recv()
            acc = acc + rb[u][t].astype(F32)
        places = UNITS[u][2]
        return acc[: places * KW * 8].reshape(places, KW, 8, BR)

    def vcopy(i, land):
        q = (p + i) % NX
        at = i if land else NX - i
        return rcopy(rprev.at[at] if land else rprev.at[0], rprev.at[at], vs_sem.at[i], vr_sem.at[at], (dp, q))

    def piece_copy(i, land):
        q = (p + i) % NX
        return rcopy(
            r3.at[q] if land else p3.at[i], r3.at[q if land else p],
            s3_sem.at[i], r3_sem.at[q if land else p], (dp, q),
        )


    def first_piece(place):
        put_piece(0, place, hbuf.at[PLACES[place]], NX)

    def cotangent(s):
        back = None
        for slot in range(NX):
            wcat = jnp.concatenate([wbuf[slot, k] for k in range(KW)], axis=1)
            part = lax.dot_general(gst[slot, s], wcat, (((1,), (1,)), ((), ())), preferred_element_type=F32)
            back = part if back is None else back + part
        g1[s, PAD : PAD + LEN, :] = (
            gbuf[0, s, PAD : PAD + LEN, :].astype(F32) + slope[s * LEN : (s + 1) * LEN, :] * back
        ).astype(BF16)

    heard(1)
    tell(2)
    second_piece(0)
    for i in range(1, NX):
        wcopy(i).wait_recv()
    heard(2)
    for step in FAR:
        send(wspread(step))
    xland(gpiece, gs_sem, gr_sem, 0)
    send(xcopy(gpiece, gs_sem, gr_sem, 5))
    xland(gpiece, gs_sem, gr_sem, 2)
    send(xcopy(gpiece, gs_sem, gr_sem, 4))
    xland(gpiece, gs_sem, gr_sem, 1)
    xland(gpiece, gs_sem, gr_sem, 3)
    for i in (0, 2, 1, 3):
        send(xcopy(hpiece, hs_sem, hr_sem, i))
    second_piece(1)
    second_piece(2)
    send(core_copy(0))
    xland(gpiece, gs_sem, gr_sem, 4)
    xland(gpiece, gs_sem, gr_sem, 5)
    second_piece(3)
    send(core_copy(1))
    to_major(0)
    @pl.loop(1, 8)
    def _(i):
        wspread_land(i)

    fetches[3].wait()
    cotangent(0)
    to_major(1)
    cotangent(1)
    stack(g1, NX, 4)
    first_piece(0)
    xland(hpiece, hs_sem, hr_sem, 0)
    send(xcopy(hpiece, hs_sem, hr_sem, 5))
    xland(hpiece, hs_sem, hr_sem, 2)
    send(xcopy(hpiece, hs_sem, hr_sem, 4))
    xland(hpiece, hs_sem, hr_sem, 1)
    first_piece(1)
    xland(hpiece, hs_sem, hr_sem, 3)
    first_piece(2)
    send(core_copy(2))
    to_minor(0)
    to_major(2)
    xland(hpiece, hs_sem, hr_sem, 4)
    xland(hpiece, hs_sem, hr_sem, 5)
    first_piece(3)
    send(core_copy(3))
    fetches[5].wait()
    for i in (2, 1, 3):
        send(vcopy(i, False))
    to_major(3)
    to_minor(1)
    to_minor(2)
    to_minor(3)
    for u in (0, 1):
        acc = minor_sum(u)
        for k in range(UNITS[u][2]):
            p3[PLACES[UNITS[u][1] + k]] = acc[k]
    for i in (2, 1, 3):
        send(piece_copy(i, False))
    rows_ref[pl.ds((NX + p) * KW, KW)] = p3[0]
    for i in range(1, NX):
        piece_copy(i, True).wait_recv()
        q = (p + i) % NX
        rows_ref[pl.ds((NX + q) * KW, KW)] = r3[q]
    for u in (2, 3):
        acc = minor_sum(u)
        for k in range(UNITS[u][2]):
            q = (p + PLACES[UNITS[u][1] + k]) % NX
            rows_ref[pl.ds(q * KW, KW)] = acc[k]

    def line(i):
        return peer_at(i // 2, b, c) - c + i % 2

    fetches[7].wait()
    for i in range(16):
        d4[i] = rows_ref[bos_ref[line(i)]]

    def group_copy(i):
        me = c * 8 + a
        return rcopy(d4.at[i], f4.at[me], fs_sem.at[i], fr_sem.at[me], (line(i), p))

    for step in FAR:
        for core in range(2):
            send(group_copy((a + step) % 8 * 2 + core))
    send(group_copy(a * 2 + 1 - c))
    f4[c * 8 + a] = d4[a * 2 + c]

    @pl.loop(1, 16)
    def _(j):
        i = (c * 8 + a + j) % 16
        rcopy(f4.at[i], f4.at[i], fs_sem.at[i], fr_sem.at[i], (sib, p)).wait_recv()

    tiles[0] = f4[...].reshape(BR, BR).astype(BF16)

    def tile_copy(i, land):
        q = (p + i) % NX
        at = i if land else NX - i
        return rcopy(tiles.at[at] if land else tiles.at[0], tiles.at[at], ts_sem.at[i], tr_sem.at[at], (dp, q))

    for i in (2, 1, 3):
        tile_copy(i, False).start()
    drain()
    sent.clear()
    sent.extend(tile_copy(i, False) for i in (2, 1, 3))
    for i in range(1, NX):
        vcopy(i, True).wait_recv()
    fetches[4].wait()
    fetches[8].wait()
    for i in range(1, NX):
        tile_copy(i, True).wait_recv()

    tile = [tiles[i] for i in range(NX)]
    left_sum = None
    stats = []
    for i in range(NX):
        part = lax.dot_general(tile[i], tile[i], (((1,), (1,)), ((), ())), preferred_element_type=F32)
        left_sum = part if left_sum is None else left_sum + part
        gram = lax.dot_general(tile[i], tile[i], (((0,), (0,)), ((), ())), preferred_element_type=F32)
        stats.append(DECAY * rprev[i] + (1.0 - DECAY) * gram)
    stats.append(DECAY * lprev_ref[...] + (1.0 - DECAY) * left_sum)
    roots = [split(r) for r in inverse_fourth_roots(stats)]
    left_root = roots[NX]
    zero = jnp.zeros((BR, BR), BF16)
    mixed = split(mm(left_root, (tile[0], zero)) + mm((tile[0], zero), roots[0]))
    raw = mm(left_root, mixed) + mm(mixed, roots[0])
    squares = raw * raw
    for i in range(1, NX):
        mixed = (bdot(left_root[0], tile[i]) + bdot(tile[i], roots[i][0])).astype(BF16)
        other = bdot(left_root[0], mixed) + bdot(mixed, roots[i][0])
        squares = squares + other * other
    total = jnp.sum(squares, axis=(0, 1), keepdims=True)
    inv = 1.0 / jnp.sqrt(total / (NX * BR * BR) + 1e-6)
    out_ref[...] = jnp.where(cnt_ref[0] > 0, raw * inv, 0.0)

    drain()


def local(
    block_input, block_middle, out_grad, lengths, conv_weight, block_of_slot, slot_count, left_prev, right_prev
):
    vmem = pl.BlockSpec(memory_space=pltpu.VMEM)
    hbm = pl.BlockSpec(memory_space=pltpu.HBM)
    dma = pltpu.SemaphoreType.DMA
    out = pl.pallas_call(
        kernel,
        out_shape=jax.ShapeDtypeStruct((BR, BR), F32),
        in_specs=[hbm] * 9,
        out_specs=vmem,
        scratch_shapes=[
            pltpu.SMEM((NS,), jnp.int32),
            pltpu.SMEM((BR,), jnp.int32),
            pltpu.SMEM((1,), jnp.int32),
            pltpu.VMEM((NS * LEN, BR), BF16),
            pltpu.VMEM((NS * LEN, BR), BF16),
            pltpu.VMEM((NS * LEN, BR), BF16),
            pltpu.VMEM((BR, BR), F32),
            pltpu.VMEM((NX, BR, BR), F32),
            pltpu.VMEM((NX, NS, LEN + 2 * PAD, BR), BF16),
            pltpu.VMEM((NX, NS, BR, LEN), BF16),
            pltpu.VMEM((NS, BR, LEN), BF16),
            pltpu.VMEM((NS * LEN, BR), F32),
            pltpu.VMEM((NX, KW, BR, BR), BF16),
            pltpu.VMEM((NX + 1, NS, LEN, KW * BR), BF16),
            pltpu.VMEM((NS, LEN + 2 * PAD, BR), BF16),
            pltpu.VMEM((2, NX, KW * BR, BR), F32),
            *[pltpu.VMEM((n * KW, 64, BR), F32) for _, _, n in UNITS],
            *[pltpu.VMEM((8, padded_rows(n), BR), BF16) for _, _, n in UNITS],
            *[pltpu.VMEM((8, padded_rows(n), BR), BF16) for _, _, n in UNITS],
            *[pltpu.VMEM((padded_rows(n), BR), BF16) for _, _, n in UNITS],
            *[pltpu.VMEM((8, padded_rows(n), BR), BF16) for _, _, n in UNITS],
            pltpu.VMEM((NX, KW, 8, BR), F32),
            pltpu.VMEM((NX, KW, 8, BR), F32),
            pltpu.VMEM((2 * NX * KW, 8, BR), F32),
            pltpu.VMEM((16, 8, BR), F32),
            pltpu.VMEM((16, 8, BR), F32),
            pltpu.VMEM((NX, BR, BR), BF16),
            dma((6,)), dma((6,)), dma((6,)), dma((6,)), dma((NX,)), dma((NX,)), dma((8,)), dma((8,)), dma((8,)),
            dma((4, 8)), dma((4, 8)), dma((4, 8)), dma((4, 8)), dma((NX,)), dma((NX,)),
            dma((16,)), dma((16,)), dma((NX,)), dma((NX,)), dma((NX,)), dma((NX,)), dma((9,)),
            pltpu.SemaphoreType.REGULAR((3,)),
        ],
        compiler_params=pltpu.CompilerParams(
            collective_id=0, has_side_effects=True, vmem_limit_bytes=60 * 1024 * 1024
        ),
    )(
        block_input, block_middle, out_grad, lengths, conv_weight.transpose(1, 0, 2), block_of_slot,
        slot_count, left_prev.reshape(BR, BR), right_prev.reshape(BR, BR),
    )
    return out.reshape(1, BR * BR)


def solution(mesh):
    return jax.shard_map(
        local,
        mesh=mesh,
        in_specs=(
            P("dp", "owner"), P("dp", "owner"), P("dp", "owner"), P("dp"), P(None, None, "owner"), P(),
            P("dp"), P("dp", None), P("dp", "owner"),
        ),
        out_specs=P("dp", "owner"),
        check_vma=False,
    )
```

```python
import jax
import jax.numpy as jnp
from jax import lax
from jax.experimental import pallas as pl
from jax.experimental.pallas import tpu as pltpu
from jax.sharding import PartitionSpec as P

MESH = pl.DeviceIdType.MESH
F32, BF16 = jnp.float32, jnp.bfloat16
KW = 5
BR = 128
LEN = 512
PAD = 16
NS = 2
NX, NY, NZ = 4, 8, 8
ITERS = 8
DECAY = 0.9


def split(a):
    high = a.astype(BF16)
    return high, (a - high.astype(F32)).astype(BF16)


def mm(a, b):
    (ah, al), (bh, bl) = a, b
    left = jnp.concatenate([ah, al], axis=1)
    right = jnp.concatenate(
        [jnp.concatenate([bh, bl], axis=1), jnp.concatenate([bh, jnp.zeros_like(bl)], axis=1)], axis=0
    )
    both = jnp.dot(left, right, preferred_element_type=F32)
    return both[:, :BR] + both[:, BR:]


def bdot(a, b):
    return jnp.dot(a, b, preferred_element_type=F32)


def inverse_fourth_roots(stats):
    rows = lax.broadcasted_iota(jnp.int32, (BR, BR), 0)
    cols = lax.broadcasted_iota(jnp.int32, (BR, BR), 1)
    eye = (rows == cols).astype(F32)
    norms = [jnp.sqrt(jnp.sum(s * s, axis=(0, 1), keepdims=True)) for s in stats]
    cur = [s / n for s, n in zip(stats, norms)]
    root = None
    for it in range(ITERS):
        fac = [1.25 * eye - 0.25 * m for m in cur]
        parts = [split(f) for f in fac]
        if it < ITERS - 1:
            square = [split(mm(f, f)) for f in parts]
            half = [split(mm(s, split(m))) for s, m in zip(square, cur)]
            cur = [mm(h, s) for h, s in zip(half, square)]
        root = fac if it == 0 else [mm(split(r), f) for r, f in zip(root, parts)]
    scale = [1.0 / jnp.sqrt(jnp.sqrt(n)) for n in norms]
    return [r * s for r, s in zip(root, scale)]


def peer_at(major, minor, core):
    z = major + core * (minor - major)
    y = minor + core * (major - minor)
    return (z * NY + y) * 2 + core


PLACES = (0, 3, 1, 2)
UNITS = ((1, 0, 3), (1, 3, 1), (0, 0, 3), (0, 3, 1))
FAR = (4, 3, 5, 2, 6, 1, 7)


def padded_rows(places):
    return -(-places * KW * 8 // 16) * 16


def kernel(
    x1_hbm, x2_hbm, g_hbm, len_hbm, w_ref, bos_hbm, cnt_hbm, lprev_hbm, rprev_hbm, out_ref,
    len_ref, bos_ref, cnt_ref, x1_ref, x2_ref, g_ref, lprev_ref, rprev,
    gbuf, hbuf, h2t, slope, wbuf, gst, g1, kbuf,
    c0, c1, c2, c3, pa0, pa1, pa2, pa3, ra0, ra1, ra2, ra3, pb0, pb1, pb2, pb3, rb0, rb1, rb2, rb3, p3, r3, rows_ref, d4, f4, tiles,
    gs_sem, gr_sem, hs_sem, hr_sem, ws_sem, wr_sem, as_sem, ar_sem, c0_sem, s1_sem, r1_sem, s2_sem, r2_sem,
    s3_sem, r3_sem, fs_sem, fr_sem, vs_sem, vr_sem, ts_sem, tr_sem, in_sem, word_sem,
):
    dp, p = lax.axis_index("dp"), lax.axis_index("owner")
    c = dp % 2
    right, left = (p + 1) % NX, (p + 3) % NX
    y = (dp // 2) % NY
    z = dp // (2 * NY)
    a = z + c * (y - z)
    b = y + c * (z - y)
    core_in, pa, ra = (c0, c1, c2, c3), (pa0, pa1, pa2, pa3), (ra0, ra1, ra2, ra3)
    pb, rb = (pb0, pb1, pb2, pb3), (rb0, rb1, rb2, rb3)

    barrier = pltpu.get_barrier_semaphore()

    def greet(dev):
        pl.semaphore_signal(barrier, inc=1, device_id=dev, device_id_type=MESH)

    near = [((z * NY + (y + step) % NY) * 2 + c, p) for step in (1, 7)]
    near += [((((z + step) % NZ) * NY + y) * 2 + c, p) for step in (1, 7)]
    near += [(dp, right), (dp, left)]
    for dev in near:
        greet(dev)
    greet((dp + 1 - 2 * c, p))

    def tell(k):
        for dev in near:
            pl.semaphore_signal(word_sem.at[k], inc=1, device_id=dev, device_id_type=MESH)

    def heard(k):
        pl.semaphore_wait(word_sem.at[k], 6)

    def rcopy(src, dst, ss, rs, dev):
        return pltpu.make_async_remote_copy(
            src_ref=src, dst_ref=dst, send_sem=ss, recv_sem=rs, device_id=dev, device_id_type=MESH
        )

    def fetch(i, src, dst):
        return pltpu.make_async_copy(src, dst, in_sem.at[i])

    own = pl.ds(pl.multiple_of(p * BR, BR), BR)
    fetches = [
        fetch(0, g_hbm, g_ref), fetch(1, x1_hbm, x1_ref), fetch(2, x2_hbm, x2_ref),
        fetch(3, w_ref.at[:, own, :], wbuf.at[0]), fetch(4, lprev_hbm, lprev_ref), fetch(5, rprev_hbm, rprev.at[0]),
        fetch(6, len_hbm, len_ref), fetch(7, bos_hbm, bos_ref), fetch(8, cnt_hbm, cnt_ref),
    ]
    for i in (6, 0, 1, 2, 3, 4, 5, 7, 8):
        fetches[i].start()

    sent = []

    def send(copy):
        copy.start()
        sent.append(copy)

    def drain():
        for copy in sent:
            copy.wait_send()

    zpad = jnp.zeros((PAD, BR), BF16)
    for slot in range(NX):
        for s in range(NS):
            gbuf[slot, s, 0:PAD, :] = zpad
            gbuf[slot, s, PAD + LEN : PAD + LEN + PAD, :] = zpad
    for s in range(NS):
        g1[s, 0:PAD, :] = zpad
        g1[s, PAD + LEN : PAD + LEN + PAD, :] = zpad
    tok = lax.broadcasted_iota(jnp.int32, (LEN, BR), 0)
    fetches[6].wait()
    fetches[0].wait()
    for s in range(NS):
        v = g_ref[s * LEN : (s + 1) * LEN, :].astype(F32)
        gbuf[0, s, PAD : PAD + LEN, :] = jnp.where(tok < len_ref[s], v, 0.0).astype(BF16)

    pl.semaphore_wait(barrier, 4 + 2 + 1)

    def gpiece(slot, s):
        return gbuf.at[slot, s, pl.ds(PAD, LEN), :]

    def hpiece(slot, s):
        return hbuf.at[slot, s]

    plan = [
        (0, 3, 1, right), (0, 3, 0, right), (0, 1, 0, left), (0, 1, 1, left),
        (1, 2, 0, left), (3, 2, 1, right),
    ]

    def xcopy(piece, ss, rs, i):
        src, dst, s, dev = plan[i]
        return rcopy(piece(src, s), piece(dst, s), ss.at[i], rs.at[i], (dp, dev))

    def xland(piece, ss, rs, i):
        src, dst, s, dev = plan[i]
        rcopy(piece(dst, s), piece(dst, s), ss.at[i], rs.at[i], (dp, dev)).wait_recv()

    def wcopy(i):
        q = (p + i) % NX
        src = w_ref.at[:, pl.ds(pl.multiple_of(q * BR + a * 16, 16), 16), :]
        dst = wbuf.at[NX - i, :, pl.ds(pl.multiple_of(a * 16, 16), 16), :]
        return rcopy(src, dst, ws_sem.at[NX - i], wr_sem.at[NX - i], (dp, q))

    def wpart(t):
        return wbuf.at[pl.ds(1, NX - 1), :, pl.ds(pl.multiple_of(t * 16, 16), 16), :]

    def wspread(i):
        t = (a + i) % 8
        return rcopy(wpart(a), wpart(a), as_sem.at[t], ar_sem.at[a], (peer_at(t, b, c), p))

    def wspread_land(i):
        t = (a + i) % 8
        rcopy(wpart(t), wpart(t), as_sem.at[t], ar_sem.at[t], (peer_at(t, b, c), p)).wait_recv()

    for i in (1, 3):
        send(wcopy(i))
    for i in (0, 2):
        send(xcopy(gpiece, gs_sem, gr_sem, i))

    tell(0)

    fetches[1].wait()

    @pl.loop(0, NS * LEN // BR)
    def _(i):
        s = i // (LEN // BR)
        t0 = pl.multiple_of((i % (LEN // BR)) * BR, BR)
        r0 = pl.multiple_of(i * BR, BR)
        valid = (lax.broadcasted_iota(jnp.int32, (BR, BR), 0) + t0 < len_ref[s]).astype(F32)
        x = x1_ref[pl.ds(r0, BR), :].astype(F32)
        h = x * (0.5 * (1.0 + lax.erf(x * 0.7071067811865476))) * valid
        hbuf[0, s, :, pl.ds(t0, BR)] = h.T.astype(BF16)

    heard(0)
    send(wcopy(2))
    for i in (1, 3):
        send(xcopy(gpiece, gs_sem, gr_sem, i))
    tell(1)
    fetches[2].wait()

    @pl.loop(0, NS * LEN // BR)
    def _(i):
        s = i // (LEN // BR)
        t0 = pl.multiple_of((i % (LEN // BR)) * BR, BR)
        r0 = pl.multiple_of(i * BR, BR)
        valid = (lax.broadcasted_iota(jnp.int32, (BR, BR), 0) + t0 < len_ref[s]).astype(F32)
        x = x2_ref[pl.ds(r0, BR), :].astype(F32)
        phi = 0.5 * (1.0 + lax.erf(x * 0.7071067811865476))
        h2t[s, :, pl.ds(t0, BR)] = (x * phi * valid).T.astype(BF16)
        slope[pl.ds(r0, BR), :] = (phi + x * jnp.exp(-0.5 * x * x) * 0.3989422804014327) * valid

    def stack(src, slot, dilation):
        for s in range(NS):
            for k in range(KW):
                r0 = PAD - (k - KW // 2) * dilation
                gst[slot, s, :, k * BR : (k + 1) * BR] = src[s, r0 : r0 + LEN, :]

    def put_piece(kk, place, acts, slot):
        prod = jnp.dot(acts[0], gst[slot, 0], preferred_element_type=F32)
        prod += jnp.dot(acts[1], gst[slot, 1], preferred_element_type=F32)
        for k in range(KW):
            kbuf[kk, place, pl.ds(k, BR, stride=KW), :] = prod[:, k * BR : (k + 1) * BR]

    def second_piece(place):
        stack(gbuf.at[PLACES[place]], PLACES[place], 8)
        put_piece(1, place, h2t, PLACES[place])

    sib = dp + 1 - 2 * c

    def ktile(u):
        kk, first, places = UNITS[u]
        return kbuf.at[kk].reshape(NX * KW, BR, BR).at[pl.ds(first * KW, places * KW)]

    def core_copy(u):
        other = pl.ds(pl.multiple_of((1 - c) * 64, 64), 64)
        return rcopy(
            ktile(u).at[:, other, :], core_in[u], c0_sem.at[2 * u], c0_sem.at[2 * u + 1], (sib, p)
        )

    def major_copy(u, t, land):
        return rcopy(
            ra[u].at[t] if land else pa[u].at[t], ra[u].at[t if land else a],
            s1_sem.at[u, t], r1_sem.at[u, t if land else a], (peer_at(t, b, c), p),
        )

    def minor_copy(u, t, land):
        return rcopy(
            rb[u].at[t] if land else pb[u], rb[u].at[t if land else b],
            s2_sem.at[u, t], r2_sem.at[u, t if land else b], (peer_at(a, t, c), p),
        )

    def to_major(u):
        core_copy(u).wait_recv()
        rows = UNITS[u][2] * KW * 8
        mine = pl.multiple_of(c * 64, 64)

        def fill(t):
            t8 = pl.multiple_of(t * 8, 8)
            both = ktile(u)[:, pl.ds(mine + t8, 8), :] + core_in[u][:, pl.ds(t8, 8), :]
            both = both.reshape(rows, BR)
            if padded_rows(UNITS[u][2]) > rows:
                both = jnp.concatenate([both, jnp.zeros((8, BR), F32)], axis=0)
            pa[u][t] = both.astype(BF16)

        for step in FAR:
            t = (a + step) % 8
            fill(t)
            send(major_copy(u, t, False))
        fill(a)

    def to_minor(u):
        acc = pa[u][a].astype(F32)
        for i in range(1, 8):
            t = (a + i) % 8
            major_copy(u, t, True).wait_recv()
            acc = acc + ra[u][t].astype(F32)
        pb[u][...] = acc.astype(BF16)

        for step in FAR:
            send(minor_copy(u, (b + step) % 8, False))

    def minor_sum(u):
        acc = pb[u][...].astype(F32)
        for i in range(1, 8):
            t = (b + i) % 8
            minor_copy(u, t, True).wait_recv()
            acc = acc + rb[u][t].astype(F32)
        places = UNITS[u][2]
        return acc[: places * KW * 8].reshape(places, KW, 8, BR)

    def vcopy(i, land):
        q = (p + i) % NX
        at = i if land else NX - i
        return rcopy(rprev.at[at] if land else rprev.at[0], rprev.at[at], vs_sem.at[i], vr_sem.at[at], (dp, q))

    def piece_copy(i, land):
        q = (p + i) % NX
        return rcopy(
            r3.at[q] if land else p3.at[i], r3.at[q if land else p],
            s3_sem.at[i], r3_sem.at[q if land else p], (dp, q),
        )


    def first_piece(place):
        put_piece(0, place, hbuf.at[PLACES[place]], NX)

    def cotangent(s):
        back = None
        for slot in range(NX):
            wcat = jnp.concatenate([wbuf[slot, k] for k in range(KW)], axis=1)
            part = lax.dot_general(gst[slot, s], wcat, (((1,), (1,)), ((), ())), preferred_element_type=F32)
            back = part if back is None else back + part
        g1[s, PAD : PAD + LEN, :] = (
            gbuf[0, s, PAD : PAD + LEN, :].astype(F32) + slope[s * LEN : (s + 1) * LEN, :] * back
        ).astype(BF16)

    heard(1)
    tell(2)
    second_piece(0)
    for i in range(1, NX):
        wcopy(i).wait_recv()
    heard(2)
    for step in FAR:
        send(wspread(step))
    xland(gpiece, gs_sem, gr_sem, 0)
    send(xcopy(gpiece, gs_sem, gr_sem, 5))
    xland(gpiece, gs_sem, gr_sem, 2)
    send(xcopy(gpiece, gs_sem, gr_sem, 4))
    for i in (0, 2):
        send(xcopy(hpiece, hs_sem, hr_sem, i))
    xland(gpiece, gs_sem, gr_sem, 1)
    xland(gpiece, gs_sem, gr_sem, 3)
    for i in (1, 3):
        send(xcopy(hpiece, hs_sem, hr_sem, i))
    second_piece(1)
    second_piece(2)
    send(core_copy(0))
    xland(gpiece, gs_sem, gr_sem, 4)
    xland(gpiece, gs_sem, gr_sem, 5)
    second_piece(3)
    send(core_copy(1))
    to_major(0)
    @pl.loop(1, 8)
    def _(i):
        wspread_land(i)

    fetches[3].wait()
    cotangent(0)
    to_major(1)
    cotangent(1)
    stack(g1, NX, 4)
    first_piece(0)
    xland(hpiece, hs_sem, hr_sem, 0)
    send(xcopy(hpiece, hs_sem, hr_sem, 5))
    xland(hpiece, hs_sem, hr_sem, 2)
    send(xcopy(hpiece, hs_sem, hr_sem, 4))
    xland(hpiece, hs_sem, hr_sem, 1)
    first_piece(1)
    xland(hpiece, hs_sem, hr_sem, 3)
    first_piece(2)
    send(core_copy(2))
    to_minor(0)
    to_major(2)
    xland(hpiece, hs_sem, hr_sem, 4)
    xland(hpiece, hs_sem, hr_sem, 5)
    first_piece(3)
    send(core_copy(3))
    fetches[5].wait()
    for i in (2, 1, 3):
        send(vcopy(i, False))
    to_major(3)
    to_minor(1)
    to_minor(2)
    to_minor(3)
    for u in (0, 1):
        acc = minor_sum(u)
        for k in range(UNITS[u][2]):
            p3[PLACES[UNITS[u][1] + k]] = acc[k]
    for i in (2, 1, 3):
        send(piece_copy(i, False))
    rows_ref[pl.ds((NX + p) * KW, KW)] = p3[0]
    for i in range(1, NX):
        piece_copy(i, True).wait_recv()
        q = (p + i) % NX
        rows_ref[pl.ds((NX + q) * KW, KW)] = r3[q]
    for u in (2, 3):
        acc = minor_sum(u)
        for k in range(UNITS[u][2]):
            q = (p + PLACES[UNITS[u][1] + k]) % NX
            rows_ref[pl.ds(q * KW, KW)] = acc[k]

    def line(i):
        return peer_at(i // 2, b, c) - c + i % 2

    fetches[7].wait()
    for i in range(16):
        d4[i] = rows_ref[bos_ref[line(i)]]

    def group_copy(i):
        me = c * 8 + a
        return rcopy(d4.at[i], f4.at[me], fs_sem.at[i], fr_sem.at[me], (line(i), p))

    for step in FAR:
        for core in range(2):
            send(group_copy((a + step) % 8 * 2 + core))
    send(group_copy(a * 2 + 1 - c))
    f4[c * 8 + a] = d4[a * 2 + c]

    @pl.loop(1, 16)
    def _(j):
        i = (c * 8 + a + j) % 16
        rcopy(f4.at[i], f4.at[i], fs_sem.at[i], fr_sem.at[i], (sib, p)).wait_recv()

    tiles[0] = f4[...].reshape(BR, BR).astype(BF16)

    def tile_copy(i, land):
        q = (p + i) % NX
        at = i if land else NX - i
        return rcopy(tiles.at[at] if land else tiles.at[0], tiles.at[at], ts_sem.at[i], tr_sem.at[at], (dp, q))

    for i in (2, 1, 3):
        tile_copy(i, False).start()
    drain()
    sent.clear()
    sent.extend(tile_copy(i, False) for i in (2, 1, 3))
    for i in range(1, NX):
        vcopy(i, True).wait_recv()
    fetches[4].wait()
    fetches[8].wait()
    for i in range(1, NX):
        tile_copy(i, True).wait_recv()

    tile = [tiles[i] for i in range(NX)]
    left_sum = None
    stats = []
    for i in range(NX):
        part = lax.dot_general(tile[i], tile[i], (((1,), (1,)), ((), ())), preferred_element_type=F32)
        left_sum = part if left_sum is None else left_sum + part
        gram = lax.dot_general(tile[i], tile[i], (((0,), (0,)), ((), ())), preferred_element_type=F32)
        stats.append(DECAY * rprev[i] + (1.0 - DECAY) * gram)
    stats.append(DECAY * lprev_ref[...] + (1.0 - DECAY) * left_sum)
    roots = [split(r) for r in inverse_fourth_roots(stats)]
    left_root = roots[NX]
    zero = jnp.zeros((BR, BR), BF16)
    mixed = split(mm(left_root, (tile[0], zero)) + mm((tile[0], zero), roots[0]))
    raw = mm(left_root, mixed) + mm(mixed, roots[0])
    squares = raw * raw
    for i in range(1, NX):
        mixed = (bdot(left_root[0], tile[i]) + bdot(tile[i], roots[i][0])).astype(BF16)
        other = bdot(left_root[0], mixed) + bdot(mixed, roots[i][0])
        squares = squares + other * other
    total = jnp.sum(squares, axis=(0, 1), keepdims=True)
    inv = 1.0 / jnp.sqrt(total / (NX * BR * BR) + 1e-6)
    out_ref[...] = jnp.where(cnt_ref[0] > 0, raw * inv, 0.0)

    drain()


def local(
    block_input, block_middle, out_grad, lengths, conv_weight, block_of_slot, slot_count, left_prev, right_prev
):
    vmem = pl.BlockSpec(memory_space=pltpu.VMEM)
    hbm = pl.BlockSpec(memory_space=pltpu.HBM)
    dma = pltpu.SemaphoreType.DMA
    out = pl.pallas_call(
        kernel,
        out_shape=jax.ShapeDtypeStruct((BR, BR), F32),
        in_specs=[hbm] * 9,
        out_specs=vmem,
        scratch_shapes=[
            pltpu.SMEM((NS,), jnp.int32),
            pltpu.SMEM((BR,), jnp.int32),
            pltpu.SMEM((1,), jnp.int32),
            pltpu.VMEM((NS * LEN, BR), BF16),
            pltpu.VMEM((NS * LEN, BR), BF16),
            pltpu.VMEM((NS * LEN, BR), BF16),
            pltpu.VMEM((BR, BR), F32),
            pltpu.VMEM((NX, BR, BR), F32),
            pltpu.VMEM((NX, NS, LEN + 2 * PAD, BR), BF16),
            pltpu.VMEM((NX, NS, BR, LEN), BF16),
            pltpu.VMEM((NS, BR, LEN), BF16),
            pltpu.VMEM((NS * LEN, BR), F32),
            pltpu.VMEM((NX, KW, BR, BR), BF16),
            pltpu.VMEM((NX + 1, NS, LEN, KW * BR), BF16),
            pltpu.VMEM((NS, LEN + 2 * PAD, BR), BF16),
            pltpu.VMEM((2, NX, KW * BR, BR), F32),
            *[pltpu.VMEM((n * KW, 64, BR), F32) for _, _, n in UNITS],
            *[pltpu.VMEM((8, padded_rows(n), BR), BF16) for _, _, n in UNITS],
            *[pltpu.VMEM((8, padded_rows(n), BR), BF16) for _, _, n in UNITS],
            *[pltpu.VMEM((padded_rows(n), BR), BF16) for _, _, n in UNITS],
            *[pltpu.VMEM((8, padded_rows(n), BR), BF16) for _, _, n in UNITS],
            pltpu.VMEM((NX, KW, 8, BR), F32),
            pltpu.VMEM((NX, KW, 8, BR), F32),
            pltpu.VMEM((2 * NX * KW, 8, BR), F32),
            pltpu.VMEM((16, 8, BR), F32),
            pltpu.VMEM((16, 8, BR), F32),
            pltpu.VMEM((NX, BR, BR), BF16),
            dma((6,)), dma((6,)), dma((6,)), dma((6,)), dma((NX,)), dma((NX,)), dma((8,)), dma((8,)), dma((8,)),
            dma((4, 8)), dma((4, 8)), dma((4, 8)), dma((4, 8)), dma((NX,)), dma((NX,)),
            dma((16,)), dma((16,)), dma((NX,)), dma((NX,)), dma((NX,)), dma((NX,)), dma((9,)),
            pltpu.SemaphoreType.REGULAR((3,)),
        ],
        compiler_params=pltpu.CompilerParams(
            collective_id=0, has_side_effects=True, vmem_limit_bytes=60 * 1024 * 1024
        ),
    )(
        block_input, block_middle, out_grad, lengths, conv_weight.transpose(1, 0, 2), block_of_slot,
        slot_count, left_prev.reshape(BR, BR), right_prev.reshape(BR, BR),
    )
    return out.reshape(1, BR * BR)


def solution(mesh):
    return jax.shard_map(
        local,
        mesh=mesh,
        in_specs=(
            P("dp", "owner"), P("dp", "owner"), P("dp", "owner"), P("dp"), P(None, None, "owner"), P(),
            P("dp"), P("dp", None), P("dp", "owner"),
        ),
        out_specs=P("dp", "owner"),
        check_vma=False,
    )
```
